256 devices in a mesh: edge: 32 (over z, x), bucket: 8 (over y, core).
Axes of the slice: x: 4, y: 4, z: 8, core: 2. Of those that a mesh axis runs over, the one named last changes fastest.
Arguments:
- unit_cost: float32 [256, 131072], P('bucket', 'edge'), may hold values from 0.2 to 2
- upper_bound: float32 [256, 131072], P('bucket', 'edge'), may hold values from 0.5 to 4
- start_primal: float32 [256, 131072], P('bucket', 'edge'), may hold values from 0 to 2
- start_dual: float32 [256, 8192], P('bucket', 'edge'), may hold values from -6 to 6
- net_target: float32 [256, 8192], P('bucket', 'edge'), may hold values from -12 to 12
- owners: int32 [131072, 2], P('edge'), may hold values from 0 to 31, all different within a row; in each aligned block of 4096 rows (0 to 4095, 4096 to 8191, ...) at most 512 rows name the same one
- local_ids: int32 [131072, 2], P('edge'), may hold values from 0 to 255
Outputs:
- primal: float32 [256, 131072], P('bucket', 'edge')
- duals: float32 [256, 8192], P('bucket', 'edge')
- totals: float32 [2, 3, 256], P(None, None, 'bucket')
The draws below stay inside these ranges and needn't reach their ends.
Inputs may be any that keep to these rules, and one draw needn't show every extreme that they name: The two owners of an edge differ. Of the edges of one index of edge, at most 512 name any one owner, and in every draw some owner is named by exactly 512 of them.
All inputs are finite; a program needn't handle non-finite values.
Results may differ from the reference program's by a relative error of at most 0.0001.
Values sent between devices are 32-bit elements; how exact they have to be, the bound alone decides.
A program may use at most 128 MiB of HBM per device.

```python
import math
import jax
import jax.numpy as jnp
import numpy as np

BUCKETS = 256
E_DEV = 4096
ACC_DEV = 256
ITERS = 3
EDGES = 131072
ACCOUNTS = 8192
CAP = 512
N_EDGE = 32


def with_ends(values, own_key, smallest, high):
    longest = values.shape.index(max(values.shape))
    spots = []
    for shift in (0, 1):
        where = [jax.random.randint(jax.random.fold_in(own_key, axis), (), 0, length) for axis, length in enumerate(values.shape)]
        where[longest] = (where[longest] + shift) % values.shape[longest]
        spots.append(tuple(where))
    return values.at[spots[0]].set(smallest).at[spots[1]].set(high)


def block_levels(key, extent, split, low, top_value):
    factor_of = 1.0
    for position, parts in split:
        heights = jax.random.uniform(jax.random.fold_in(jax.random.fold_in(key, 6), position), (parts,), jnp.float32, low / len(split), top_value / len(split))
        factor_of = factor_of * jnp.repeat(jnp.exp(heights), extent[position] // parts).reshape((-1,) + (1,) * (len(extent) - 1 - position))
    return factor_of


def cumulative_ranks(amount, skew):
    weights = [(1 << 20) // math.isqrt(rank ** skew) + 1 for rank in range(1, amount + 1)]
    deviation = 1 + sum(weights) // (1 << 30)
    return np.cumsum(np.array([max(1, weight // deviation) for weight in weights]))


def skewed_ids(own_key, shape, amount, lean):
    table = cumulative_ranks(amount, lean)
    ticket = jax.random.randint(jax.random.fold_in(own_key, 1), shape, 0, int(table[amount - 1]))
    rank = jnp.searchsorted(jnp.asarray(table, jnp.int32), ticket, side="right")
    return jax.random.permutation(jax.random.fold_in(own_key, 2), amount)[rank].astype(jnp.int32)


def shared_out(own_key, own, number, rows, amount, top, bound, slope):
    order = jax.random.permutation(own_key, amount)
    packed, usual = shares(amount, rows * top, bound, slope, True), shares(amount, rows * top, bound, slope, False)
    places = jnp.arange(amount)

    def named(tallies, offset_by):
        used = int((tallies > 0).sum())
        fixed = max(1, used // 4)
        moved = fixed + (places - fixed + offset_by * (used - fixed)) % max(1, amount - fixed)
        return jnp.zeros((amount,), jnp.int32).at[order[jnp.where(places < fixed, places, moved)]].set(jnp.asarray(tallies, jnp.int32))

    tallies = jnp.where(number % 4 == 0, named(packed, number // 4), named(usual, number - number // 4 - 1))
    mixed = jax.random.permutation(jax.random.fold_in(own, 3), amount)
    donor, taker = mixed[0:amount // 2 * 2:2], mixed[1:amount // 2 * 2:2]
    room = jnp.minimum(tallies[donor] - 1, bound - tallies[taker]) // 2
    room = jnp.where((donor == order[0]) | (taker == order[0]) | (tallies[taker] == 0), 0, jnp.maximum(room, 0))
    moved = jax.random.randint(jax.random.fold_in(own, 4), (amount // 2,), 0, 1 << 20) % (room + 1)
    tallies = tallies.at[donor].add(-moved).at[taker].add(moved)
    items = jnp.searchsorted(jnp.cumsum(tallies), jnp.arange(rows * top), side="right").astype(jnp.int32)
    listing = items.reshape(top, rows).T
    listing = listing[jax.random.permutation(jax.random.fold_in(own, 1), rows)]
    offset_by = jax.random.randint(jax.random.fold_in(own, 2), (rows, 1), 0, top)
    return jnp.take_along_axis(listing, (jnp.arange(top)[None, :] + offset_by) % top, axis=1)


def shares(number_of, total, most, slope, full):
    weights = [(1 << 20) // math.isqrt(rank ** slope) + 1 for rank in range(1, number_of + 1)]
    largest = most if full else min(most, max(-(-total // number_of), total * weights[0] // sum(weights)))
    least = 1 if total - largest >= number_of - 1 else 0
    counts, rest = [largest] + [least] * (number_of - 1), total - largest - least * (number_of - 1)
    while rest > 0:
        candidates = [i for i in range(1, number_of) if counts[i] < largest] or [i for i in range(1, number_of) if counts[i] < most]
        mass, budget = sum([weights[i] for i in candidates]), rest
        for i in candidates:
            addition = min(most - counts[i], max(1, budget * weights[i] // mass), rest)
            counts[i] = counts[i] + addition
            rest = rest - addition
    return np.array(counts)


def gaussian(stream_key, dims, spread, reach, cuts=(), dtype=jnp.bfloat16):
    result = spread * jax.random.normal(stream_key, dims, jnp.float32)
    if cuts:
        result = result * block_levels(stream_key, dims, cuts, -0.22, 0.18)
    return jnp.clip(result, -reach, reach).astype(dtype)


def setup_inputs(seed: int = 0) -> dict:
    streams_of = jax.random.split(jax.random.key(seed), 8)
    unit_cost = jnp.clip(jnp.exp(math.log(2.0) - 2.3025851 * jax.random.uniform(streams_of[0], (BUCKETS, EDGES), jnp.float32) ** block_levels(streams_of[0], (BUCKETS, EDGES), ((0, 8), (1, 32)), -0.2, 0.2)), 0.2, 2.0)
    upper_bound = jnp.clip(jnp.exp(math.log(4.0) - 2.0794415 * jax.random.uniform(streams_of[1], (BUCKETS, EDGES), jnp.float32) ** block_levels(streams_of[1], (BUCKETS, EDGES), ((0, 8), (1, 32)), -0.2, 0.2)), 0.5, 4.0)
    start_primal = jnp.clip(2.0 * jax.random.uniform(streams_of[2], (BUCKETS, EDGES), jnp.float32) ** block_levels(streams_of[2], (BUCKETS, EDGES), ((0, 8), (1, 32)), -0.2, 0.2), 0.0, 2.0)
    start_dual = gaussian(streams_of[3], (BUCKETS, ACCOUNTS), 1.0, 6.0, ((0, 8), (1, 32)), jnp.float32)
    net_target = gaussian(streams_of[4], (BUCKETS, ACCOUNTS), 2.0, 12.0, ((0, 8), (1, 32)), jnp.float32)
    owners_keys = jax.random.split(jax.random.fold_in(streams_of[5], 1), EDGES // E_DEV)
    owners_turns = jax.random.permutation(jax.random.fold_in(streams_of[5], 3), EDGES // E_DEV)
    owners = jax.vmap(lambda own, number: shared_out(jax.random.fold_in(streams_of[5], 2), own, number, E_DEV, N_EDGE, 2, CAP, 2))(owners_keys, owners_turns).reshape((EDGES, 2))
    local_ids = with_ends(skewed_ids(streams_of[6], (EDGES, 2), ACC_DEV, 2), jax.random.fold_in(streams_of[6], 3), 0, ACC_DEV - 1).astype(jnp.int32)
    return dict(unit_cost=unit_cost, upper_bound=upper_bound, start_primal=start_primal, start_dual=start_dual, net_target=net_target, owners=owners, local_ids=local_ids)


def reference(unit_cost, upper_bound, start_primal, start_dual, net_target, owners, local_ids):
    source = owners[:, 0] * ACC_DEV + local_ids[:, 0]
    sink = owners[:, 1] * ACC_DEV + local_ids[:, 1]
    unit_terms = jnp.ones(source.shape, jnp.float32)
    degree = jnp.zeros((ACCOUNTS,), jnp.float32).at[source].add(unit_terms).at[sink].add(unit_terms)
    dual_step = 1.0 / jnp.maximum(degree, 1.0)
    primal, duals = start_primal, start_dual
    squares, spends = [], []
    for sweep in range(ITERS):
        pulled = duals[:, source] - duals[:, sink]
        moved = jnp.clip(primal - 0.5 * (unit_cost - pulled), 0.0, upper_bound)
        extended = 2.0 * moved - primal
        applied = jnp.zeros((BUCKETS, ACCOUNTS), jnp.float32).at[:, source].add(extended).at[:, sink].add(-extended)
        residual = net_target - applied
        duals = duals + dual_step[None, :] * residual
        primal = moved
        squares.append(jnp.sum(residual * residual, axis=1))
        spends.append(jnp.sum(unit_cost * moved, axis=1))
    totals = jnp.stack([jnp.stack(squares), jnp.stack(spends)])
    return primal, duals, totals
```

```python
import functools

import jax
import jax.numpy as jnp
from jax import lax
from jax.experimental import pallas as pl
from jax.experimental.pallas import tpu as pltpu
from jax.sharding import PartitionSpec as P

ITERS = 3
X = 4
Z = 8
CH = 8
PULL = 2048
PUSH = 4096
F32 = jnp.float32
BF16 = jnp.bfloat16


def split(value):
    high = value.astype(BF16)
    low = (value - high.astype(F32)).astype(BF16)
    return high, low


def kernel(cost_ref, bound_ref, start_ref, dual_ref, target_ref, owner_ref, local_ref,
           primal_ref, duals_ref, totals_ref,
           hot, hot_t, own_row, own_half, ext, gath, part, rsx, zsum, rsz,
           deg_part, deg_x, deg_z, step_ref, spend_ref, tot, tot_z, tot_x,
           sem_agz, sem_agx, sem_rsx, sem_rsz, sem_dx, sem_dz, sem_tz, sem_tx):
    edges = cost_ref.shape[1]
    chunks = cost_ref.shape[0] // CH
    slots = ITERS * chunks
    me = lax.axis_index("edge")
    my_x = lax.rem(me, X)
    my_z = lax.div(me, X)

    def at_x(j):
        return my_z * X + lax.rem(my_x + j, X)

    def at_z(j):
        return lax.rem(my_z + j, Z) * X + my_x

    def remote(src, dst, sems, device):
        return pltpu.make_async_remote_copy(
            src_ref=src, dst_ref=dst, send_sem=sems.at[0], recv_sem=sems.at[1],
            device_id={"edge": device}, device_id_type=pl.DeviceIdType.MESH)

    def agz(c):
        block = gath.at[c, my_x, my_z]
        return [remote(block, block, sem_agz.at[c, j - 1], at_z(j)) for j in range(1, Z)]

    def agx(c):
        block = gath.at[c, my_x]
        return [remote(block, block, sem_agx.at[c, j - 1], at_x(j)) for j in range(1, X)]

    def to_x(c):
        return [remote(part.at[c, lax.rem(my_x + j, X)], rsx.at[c, j - 1], sem_rsx.at[c, j - 1], at_x(j))
                for j in range(1, X)]

    def to_z(c):
        return [remote(zsum.at[c, lax.rem(my_z + j, Z)], rsz.at[c, j - 1], sem_rsz.at[c, j - 1], at_z(j))
                for j in range(1, Z)]

    def deg_to_x():
        return [remote(deg_part.at[lax.rem(my_x + j, X)], deg_x.at[j - 1], sem_dx.at[j - 1], at_x(j))
                for j in range(1, X)]

    def deg_to_z():
        return [remote(deg_z.at[my_z], deg_z.at[my_z], sem_dz.at[j - 1], at_z(j)) for j in range(1, Z)]

    def tot_to_z():
        return [remote(tot_z.at[my_z], tot_z.at[my_z], sem_tz.at[j - 1], at_z(j)) for j in range(1, Z)]

    def tot_to_x():
        return [remote(tot_x.at[my_x], tot_x.at[my_x], sem_tx.at[j - 1], at_x(j)) for j in range(1, X)]

    def start(copies):
        for copy in copies:
            copy.start()

    def wait(copies):
        for copy in copies:
            copy.wait()

    barrier = pltpu.get_barrier_semaphore()
    for j in range(1, Z):
        pl.semaphore_signal(barrier, inc=1, device_id={"edge": at_z(j)}, device_id_type=pl.DeviceIdType.MESH)
    for j in range(1, X):
        pl.semaphore_signal(barrier, inc=1, device_id={"edge": at_x(j)}, device_id_type=pl.DeviceIdType.MESH)
    pl.semaphore_wait(barrier, Z + X - 2)

    for c in range(chunks):
        gath[c, my_x, my_z] = dual_ref[c * CH:(c + 1) * CH, :]
        start(agz(c))

    for side in range(2):
        owner = owner_ref[side:side + 1, :]
        row = (owner & (X - 1)) * Z + (owner >> 2)
        own_row[side:side + 1, :] = row
        own_half[side] = jnp.broadcast_to(row.astype(F32), (2 * CH, edges)).astype(BF16)

        def build(j, carry):
            cols = pl.ds(pl.multiple_of(j * 256, 256), 256)
            one = (lax.broadcasted_iota(jnp.int32, (256, 256), 0) == local_ref[side:side + 1, cols]).astype(F32)
            hot[side, :, cols] = one.astype(BF16)
            hot_t[side, cols, :] = one.T.astype(BF16)
            return carry

        lax.fori_loop(0, edges // 256, build, 0)

    for c in range(chunks):
        wait(agz(c))
        start(agx(c))

    degree = None
    for side in range(2):
        rows = lax.broadcasted_iota(jnp.int32, (X * Z, edges), 0)
        named = (rows == own_row[side:side + 1, :]).astype(F32).astype(BF16)
        count = jnp.dot(named, hot_t[side], preferred_element_type=F32)
        degree = count if degree is None else degree + count
    for x in range(X):
        deg_part[x] = degree[x * Z:(x + 1) * Z]
    start(deg_to_x())

    primal_ref[...] = start_ref[...]
    duals_ref[...] = dual_ref[...]
    tot[...] = jnp.zeros_like(tot)
    lane = lax.broadcasted_iota(jnp.int32, (CH, 128), 1)

    def degree_x():
        wait(deg_to_x())
        deg_z[my_z] = deg_part[my_x] + deg_x[0] + deg_x[1] + deg_x[2]
        start(deg_to_z())

    def degree_z():
        wait(deg_to_z())
        total = deg_z[0, pl.ds(my_z, 1), :]
        for z in range(1, Z):
            total = total + deg_z[z, pl.ds(my_z, 1), :]
        step_ref[...] = jnp.broadcast_to(1.0 / jnp.maximum(total, 1.0), step_ref.shape)

    def pull(t):
        c, sweep = lax.rem(t, chunks), lax.div(t, chunks)
        rows = pl.ds(pl.multiple_of(c * CH, CH), CH)
        wait(agx(c))
        high, low = split(gath[c].reshape(X * Z, CH, 256))
        left = jnp.concatenate([high, low], axis=1).reshape(2 * X * Z * CH, 256)
        spend_ref[...] = jnp.zeros_like(spend_ref)

        def block(b, carry):
            cols = pl.ds(pl.multiple_of(b * PULL, PULL), PULL)
            ends = []
            for side in range(2):
                all_rows = jnp.dot(left, hot[side, :, cols], preferred_element_type=F32)
                owner = jnp.broadcast_to(own_row[side:side + 1, cols], (CH, PULL))
                value = jnp.zeros((CH, PULL), F32)
                for o in range(X * Z):
                    at = o * 2 * CH
                    value = jnp.where(owner == o, all_rows[at:at + CH] + all_rows[at + CH:at + 2 * CH], value)
                ends.append(value)
            pulled = ends[0] - ends[1]
            cost, primal = cost_ref[rows, cols], primal_ref[rows, cols]
            moved = jnp.minimum(jnp.maximum(primal - 0.5 * (cost - pulled), 0.0), bound_ref[rows, cols])
            extended = 2.0 * moved - primal
            primal_ref[rows, cols] = moved
            high, low = split(extended)
            both = jnp.concatenate([high, low], axis=0)
            ext[0, :, cols] = both
            ext[1, :, cols] = -both
            spend_ref[...] += jnp.sum(cost * moved, axis=1, keepdims=True)
            return carry

        lax.fori_loop(0, edges // PULL, block, 0)
        tot[rows, :] += jnp.where(lane == ITERS + sweep, jnp.broadcast_to(spend_ref[:, :1], (CH, 128)), 0.0)

    def push(t):
        c = lax.rem(t, chunks)
        total = None
        for side in range(2):
            for b in range(edges // PUSH):
                cols = slice(b * PUSH, (b + 1) * PUSH)
                value = ext[side, :, cols]
                owner = own_half[side, :, cols]
                zero = jnp.zeros_like(value)
                left = jnp.concatenate([jnp.where(owner == BF16(o), value, zero) for o in range(X * Z)], axis=0)
                term = jnp.dot(left, hot_t[side, cols, :], preferred_element_type=F32)
                total = term if total is None else total + term
        for o in range(X * Z):
            at = o * 2 * CH
            part[c, o // Z, o % Z] = total[at:at + CH] + total[at + CH:at + 2 * CH]
        start(to_x(c))

    def stage_a(t):
        c = lax.rem(t, chunks)
        wait(to_x(c))
        zsum[c] = part[c, my_x] + rsx[c, 0] + rsx[c, 1] + rsx[c, 2]
        start(to_z(c))

    def stage_b(t):
        c, sweep = lax.rem(t, chunks), lax.div(t, chunks)
        rows = pl.ds(pl.multiple_of(c * CH, CH), CH)
        wait(to_z(c))
        applied = zsum[c, my_z]
        for j in range(Z - 1):
            applied = applied + rsz[c, j]
        residual = target_ref[rows, :] - applied
        duals = duals_ref[rows, :] + step_ref[...] * residual
        duals_ref[rows, :] = duals
        square = jnp.sum(residual * residual, axis=1, keepdims=True)
        tot[rows, :] += jnp.where(lane == sweep, jnp.broadcast_to(square, (CH, 128)), 0.0)

        @pl.when(sweep < ITERS - 1)
        def _():
            gath[c, my_x, my_z] = duals
            start(agz(c))

    def stage_c(t):
        c, sweep = lax.rem(t, chunks), lax.div(t, chunks)

        @pl.when(sweep < ITERS - 1)
        def _():
            wait(agz(c))
            start(agx(c))

    def slot(t, carry):
        pull(t)

        @pl.when(t == 1)
        def _():
            degree_z()

        @pl.when(t >= 2)
        def _():
            stage_b(t - 2)

        push(t)

        @pl.when(t == 0)
        def _():
            degree_x()

        @pl.when(t >= 1)
        def _():
            stage_a(t - 1)

        @pl.when(t >= 2)
        def _():
            stage_c(t - 2)

        return carry

    lax.fori_loop(0, slots, slot, 0)
    stage_b(slots - 2)
    stage_a(slots - 1)
    stage_b(slots - 1)

    tot_z[my_z] = tot[...]
    start(tot_to_z())
    wait(tot_to_z())
    mine = tot_z[0]
    for z in range(1, Z):
        mine = mine + tot_z[z]
    tot_x[my_x] = mine
    start(tot_to_x())
    wait(tot_to_x())
    totals_ref[...] = (tot_x[0] + tot_x[1]) + (tot_x[2] + tot_x[3])


def body(unit_cost, upper_bound, start_primal, start_dual, net_target, owners, local_ids):
    buckets, edges = unit_cost.shape
    accounts = start_dual.shape[1]
    chunks = buckets // CH
    block = (CH, accounts)
    dma = pltpu.SemaphoreType.DMA
    primal, duals, totals = pl.pallas_call(
        kernel,
        out_shape=(
            jax.ShapeDtypeStruct((buckets, edges), F32),
            jax.ShapeDtypeStruct((buckets, accounts), F32),
            jax.ShapeDtypeStruct((buckets, 128), F32),
        ),
        in_specs=[pl.BlockSpec(memory_space=pltpu.VMEM)] * 7,
        out_specs=[pl.BlockSpec(memory_space=pltpu.VMEM)] * 3,
        scratch_shapes=[
            pltpu.VMEM((2, accounts, edges), BF16),
            pltpu.VMEM((2, edges, accounts), BF16),
            pltpu.VMEM((2, edges), jnp.int32),
            pltpu.VMEM((2, 2 * CH, edges), BF16),
            pltpu.VMEM((2, 2 * CH, edges), BF16),
            pltpu.VMEM((chunks, X, Z) + block, F32),
            pltpu.VMEM((chunks, X, Z) + block, F32),
            pltpu.VMEM((chunks, X - 1, Z) + block, F32),
            pltpu.VMEM((chunks, Z) + block, F32),
            pltpu.VMEM((chunks, Z - 1) + block, F32),
            pltpu.VMEM((X, Z, accounts), F32),
            pltpu.VMEM((X - 1, Z, accounts), F32),
            pltpu.VMEM((Z, Z, accounts), F32),
            pltpu.VMEM(block, F32),
            pltpu.VMEM((CH, 128), F32),
            pltpu.VMEM((buckets, 128), F32),
            pltpu.VMEM((Z, buckets, 128), F32),
            pltpu.VMEM((X, buckets, 128), F32),
            dma((chunks, Z - 1, 2)),
            dma((chunks, X - 1, 2)),
            dma((chunks, X - 1, 2)),
            dma((chunks, Z - 1, 2)),
            dma((X - 1, 2)),
            dma((Z - 1, 2)),
            dma((Z - 1, 2)),
            dma((X - 1, 2)),
        ],
        compiler_params=pltpu.CompilerParams(
            collective_id=0, has_side_effects=True, vmem_limit_bytes=56 * 2**20),
        cost_estimate=pl.CostEstimate(flops=52 * 10**9, bytes_accessed=4 * 2**20, transcendentals=0),
    )(unit_cost, upper_bound, start_primal, start_dual, net_target, owners.T, local_ids.T)
    return primal, duals, totals[:, :2 * ITERS].T.reshape(2, ITERS, buckets)


def solution(mesh):
    return jax.shard_map(
        body,
        mesh=mesh,
        in_specs=(
            P("bucket", "edge"),
            P("bucket", "edge"),
            P("bucket", "edge"),
            P("bucket", "edge"),
            P("bucket", "edge"),
            P("edge", None),
            P("edge", None),
        ),
        out_specs=(P("bucket", "edge"), P("bucket", "edge"), P(None, None, "bucket")),
        check_vma=False,
    )
```

```python
import functools

import jax
import jax.numpy as jnp
from jax import lax
from jax.experimental import pallas as pl
from jax.experimental.pallas import tpu as pltpu
from jax.sharding import PartitionSpec as P

ITERS = 3
X = 4
Z = 8
CH = 8
PULL = 2048
F32 = jnp.float32
BF16 = jnp.bfloat16


def split(value):
    high = value.astype(BF16)
    low = (value - high.astype(F32)).astype(BF16)
    return high, low


def kernel(cost_ref, bound_ref, start_ref, dual_ref, target_ref, owner_ref, local_ref,
           primal_ref, duals_ref, totals_ref,
           hot, own_row, own_half, ext, gath, part, rsx, zsum, rsz,
           deg_part, deg_x, deg_z, step_ref, tot, tot_z, tot_x,
           sem_agz, sem_agx, sem_rsx, sem_rsz, sem_dx, sem_dz, sem_tz, sem_tx):
    edges = cost_ref.shape[1]
    chunks = cost_ref.shape[0] // CH
    slots = ITERS * chunks
    me = lax.axis_index("edge")
    my_x = lax.rem(me, X)
    my_z = lax.div(me, X)

    def at_x(j):
        return my_z * X + lax.rem(my_x + j, X)

    def at_z(j):
        return lax.rem(my_z + j, Z) * X + my_x

    def remote(src, dst, sems, device):
        return pltpu.make_async_remote_copy(
            src_ref=src, dst_ref=dst, send_sem=sems.at[0], recv_sem=sems.at[1],
            device_id={"edge": device}, device_id_type=pl.DeviceIdType.MESH)

    def agz(c):
        block = gath.at[c, my_x, my_z]
        return [remote(block, block, sem_agz.at[c, j - 1], at_z(j)) for j in range(1, Z)]

    def agx(c):
        block = gath.at[c, my_x]
        return [remote(block, block, sem_agx.at[c, j - 1], at_x(j)) for j in range(1, X)]

    def to_x(c):
        return [remote(part.at[c, lax.rem(my_x + j, X)], rsx.at[c, j - 1], sem_rsx.at[c, j - 1], at_x(j))
                for j in range(1, X)]

    def to_z(c):
        return [remote(zsum.at[c, lax.rem(my_z + j, Z)], rsz.at[c, j - 1], sem_rsz.at[c, j - 1], at_z(j))
                for j in range(1, Z)]

    def deg_to_x():
        return [remote(deg_part.at[lax.rem(my_x + j, X)], deg_x.at[j - 1], sem_dx.at[j - 1], at_x(j))
                for j in range(1, X)]

    def deg_to_z():
        return [remote(deg_z.at[my_z], deg_z.at[my_z], sem_dz.at[j - 1], at_z(j)) for j in range(1, Z)]

    def tot_to_z():
        return [remote(tot_z.at[my_z], tot_z.at[my_z], sem_tz.at[j - 1], at_z(j)) for j in range(1, Z)]

    def tot_to_x():
        return [remote(tot_x.at[my_x], tot_x.at[my_x], sem_tx.at[j - 1], at_x(j)) for j in range(1, X)]

    def start(copies):
        for copy in copies:
            copy.start()

    def wait(copies):
        for copy in copies:
            copy.wait()

    barrier = pltpu.get_barrier_semaphore()
    for j in range(1, Z):
        pl.semaphore_signal(barrier, inc=1, device_id={"edge": at_z(j)}, device_id_type=pl.DeviceIdType.MESH)
    for j in range(1, X):
        pl.semaphore_signal(barrier, inc=1, device_id={"edge": at_x(j)}, device_id_type=pl.DeviceIdType.MESH)
    pl.semaphore_wait(barrier, Z + X - 2)

    for c in range(chunks):
        gath[c, my_x, my_z] = dual_ref[c * CH:(c + 1) * CH, :]
        start(agz(c))

    for side in range(2):
        owner = owner_ref[side:side + 1, :]
        row = (owner & (X - 1)) * Z + (owner >> 2)
        own_row[side:side + 1, :] = row
        own_half[side] = jnp.broadcast_to(row.astype(F32), (2 * CH, edges)).astype(BF16)

        def build(j, carry):
            cols = pl.ds(pl.multiple_of(j * 256, 256), 256)
            one = (lax.broadcasted_iota(jnp.int32, (256, 256), 0) == local_ref[side:side + 1, cols]).astype(F32)
            hot[side, :, cols] = one.astype(BF16)
            return carry

        lax.fori_loop(0, edges // 256, build, 0)

    for c in range(chunks):
        wait(agz(c))
        start(agx(c))

    degree = None
    for side in range(2):
        rows = lax.broadcasted_iota(jnp.int32, (X * Z, edges), 0)
        named = (rows == own_row[side:side + 1, :]).astype(F32).astype(BF16)
        count = lax.dot_general(named, hot[side], (((1,), (1,)), ((), ())), preferred_element_type=F32)
        degree = count if degree is None else degree + count
    for x in range(X):
        deg_part[x] = degree[x * Z:(x + 1) * Z]
    start(deg_to_x())

    primal_ref[...] = start_ref[...]
    duals_ref[...] = dual_ref[...]
    tot[...] = jnp.zeros_like(tot)
    lane = lax.broadcasted_iota(jnp.int32, (CH, 128), 1)

    def degree_x():
        wait(deg_to_x())
        deg_z[my_z] = deg_part[my_x] + deg_x[0] + deg_x[1] + deg_x[2]
        start(deg_to_z())

    def degree_z():
        wait(deg_to_z())
        total = deg_z[0, pl.ds(my_z, 1), :]
        for z in range(1, Z):
            total = total + deg_z[z, pl.ds(my_z, 1), :]
        step_ref[...] = jnp.broadcast_to(1.0 / jnp.maximum(total, 1.0), step_ref.shape)

    def lefts(c):
        high, low = split(gath[c].reshape(X * Z, CH, 256))
        return jnp.concatenate([high, low], axis=1).reshape(2 * X * Z * CH, 256)

    def pull(t, b):
        c, sweep = lax.rem(t, chunks), lax.div(t, chunks)
        rows = pl.ds(pl.multiple_of(c * CH, CH), CH)
        cols = slice(b * PULL, (b + 1) * PULL)
        left = lefts(c)
        ends = []
        for side in range(2):
            all_rows = jnp.dot(left, hot[side, :, cols], preferred_element_type=F32)
            owner = jnp.broadcast_to(own_row[side:side + 1, cols], (CH, PULL))
            value = jnp.zeros((CH, PULL), F32)
            for o in range(X * Z):
                at = o * 2 * CH
                value = jnp.where(owner == o, all_rows[at:at + CH] + all_rows[at + CH:at + 2 * CH], value)
            ends.append(value)
        pulled = ends[0] - ends[1]
        cost, primal = cost_ref[rows, cols], primal_ref[rows, cols]
        moved = jnp.minimum(jnp.maximum(primal - 0.5 * (cost - pulled), 0.0), bound_ref[rows, cols])
        extended = 2.0 * moved - primal
        primal_ref[rows, cols] = moved
        high, low = split(extended)
        both = jnp.concatenate([high, low], axis=0)
        ext[0, :, cols] = both
        ext[1, :, cols] = -both
        spend = jnp.sum(cost * moved, axis=1, keepdims=True)
        tot[rows, :] += jnp.where(lane == ITERS + sweep, jnp.broadcast_to(spend, (CH, 128)), 0.0)

    def push(t, side):
        c = lax.rem(t, chunks)
        value = ext[side]
        owner = own_half[side]
        zero = jnp.zeros_like(value)
        left = jnp.concatenate([jnp.where(owner == BF16(o), value, zero) for o in range(X * Z)], axis=0)
        total = lax.dot_general(left, hot[side], (((1,), (1,)), ((), ())), preferred_element_type=F32)
        for o in range(X * Z):
            at = o * 2 * CH
            term = total[at:at + CH] + total[at + CH:at + 2 * CH]
            part[c, o // Z, o % Z] = term if side == 0 else part[c, o // Z, o % Z] + term
        if side == 1:
            start(to_x(c))

    def stage_a(t):
        c = lax.rem(t, chunks)
        wait(to_x(c))
        zsum[c] = part[c, my_x] + rsx[c, 0] + rsx[c, 1] + rsx[c, 2]
        start(to_z(c))

    def stage_b(t):
        c, sweep = lax.rem(t, chunks), lax.div(t, chunks)
        rows = pl.ds(pl.multiple_of(c * CH, CH), CH)
        wait(to_z(c))
        applied = zsum[c, my_z]
        for j in range(Z - 1):
            applied = applied + rsz[c, j]
        residual = target_ref[rows, :] - applied
        duals = duals_ref[rows, :] + step_ref[...] * residual
        duals_ref[rows, :] = duals
        square = jnp.sum(residual * residual, axis=1, keepdims=True)
        tot[rows, :] += jnp.where(lane == sweep, jnp.broadcast_to(square, (CH, 128)), 0.0)

        @pl.when(sweep < ITERS - 1)
        def _():
            gath[c, my_x, my_z] = duals
            start(agz(c))

    def stage_c(t):
        c, sweep = lax.rem(t, chunks), lax.div(t, chunks)

        @pl.when(sweep < ITERS - 1)
        def _():
            wait(agz(c))
            start(agx(c))

    def slot(t, carry):
        wait(agx(lax.rem(t, chunks)))
        pull(t, 0)

        @pl.when(t >= 3)
        def _():
            stage_c(t - 3)

        pull(t, 1)

        @pl.when(t == 1)
        def _():
            degree_z()

        @pl.when(t >= 2)
        def _():
            stage_b(t - 2)

        push(t, 0)

        @pl.when(t == 0)
        def _():
            degree_x()

        @pl.when(t >= 1)
        def _():
            stage_a(t - 1)

        push(t, 1)
        return carry

    lax.fori_loop(0, slots, slot, 0)
    stage_b(slots - 2)
    stage_a(slots - 1)
    stage_b(slots - 1)

    tot_z[my_z] = tot[...].T[:8]
    start(tot_to_z())
    wait(tot_to_z())
    mine = tot_z[0]
    for z in range(1, Z):
        mine = mine + tot_z[z]
    tot_x[my_x] = mine
    start(tot_to_x())
    wait(tot_to_x())
    mine = (tot_x[0] + tot_x[1]) + (tot_x[2] + tot_x[3])
    for i in range(ITERS):
        totals_ref[i, 0:1, :] = mine[i:i + 1, :totals_ref.shape[2]]
        totals_ref[i, 1:2, :] = mine[ITERS + i:ITERS + i + 1, :totals_ref.shape[2]]


def body(unit_cost, upper_bound, start_primal, start_dual, net_target, owners, local_ids):
    buckets, edges = unit_cost.shape
    accounts = start_dual.shape[1]
    chunks = buckets // CH
    block = (CH, accounts)
    dma = pltpu.SemaphoreType.DMA
    primal, duals, totals = pl.pallas_call(
        kernel,
        out_shape=(
            jax.ShapeDtypeStruct((buckets, edges), F32),
            jax.ShapeDtypeStruct((buckets, accounts), F32),
            jax.ShapeDtypeStruct((ITERS, 2, buckets), F32),
        ),
        in_specs=[pl.BlockSpec(memory_space=pltpu.VMEM)] * 7,
        out_specs=[pl.BlockSpec(memory_space=pltpu.VMEM)] * 3,
        scratch_shapes=[
            pltpu.VMEM((2, accounts, edges), BF16),
            pltpu.VMEM((2, edges), jnp.int32),
            pltpu.VMEM((2, 2 * CH, edges), BF16),
            pltpu.VMEM((2, 2 * CH, edges), BF16),
            pltpu.VMEM((chunks, X, Z) + block, F32),
            pltpu.VMEM((chunks, X, Z) + block, F32),
            pltpu.VMEM((chunks, X - 1, Z) + block, F32),
            pltpu.VMEM((chunks, Z) + block, F32),
            pltpu.VMEM((chunks, Z - 1) + block, F32),
            pltpu.VMEM((X, Z, accounts), F32),
            pltpu.VMEM((X - 1, Z, accounts), F32),
            pltpu.VMEM((Z, Z, accounts), F32),
            pltpu.VMEM(block, F32),
            pltpu.VMEM((128, 128), F32),
            pltpu.VMEM((Z, 8, 128), F32),
            pltpu.VMEM((X, 8, 128), F32),
            dma((chunks, Z - 1, 2)),
            dma((chunks, X - 1, 2)),
            dma((chunks, X - 1, 2)),
            dma((chunks, Z - 1, 2)),
            dma((X - 1, 2)),
            dma((Z - 1, 2)),
            dma((Z - 1, 2)),
            dma((X - 1, 2)),
        ],
        compiler_params=pltpu.CompilerParams(
            collective_id=0, has_side_effects=True, vmem_limit_bytes=56 * 2**20),
        cost_estimate=pl.CostEstimate(flops=52 * 10**9, bytes_accessed=4 * 2**20, transcendentals=0),
    )(unit_cost, upper_bound, start_primal, start_dual, net_target, owners.T, local_ids.T)
    return primal, duals, totals.transpose(1, 0, 2)


def solution(mesh):
    return jax.shard_map(
        body,
        mesh=mesh,
        in_specs=(
            P("bucket", "edge"),
            P("bucket", "edge"),
            P("bucket", "edge"),
            P("bucket", "edge"),
            P("bucket", "edge"),
            P("edge", None),
            P("edge", None),
        ),
        out_specs=(P("bucket", "edge"), P("bucket", "edge"), P(None, None, "bucket")),
        check_vma=False,
    )
```

```python
import jax
import jax.numpy as jnp
from jax import lax
from jax.experimental import pallas as pl
from jax.experimental.pallas import tpu as pltpu
from jax.sharding import PartitionSpec as P

ITERS = 3
X = 4
Z = 8
OWNERS = X * Z
HALF = 4
CHUNKS = 2
GROUP = HALF * CHUNKS
LANES = 128
F32 = jnp.float32
BF16 = jnp.bfloat16


def turn(value):
    axis = value.ndim - 2
    first = lax.slice_in_dim(value, 0, HALF, axis=axis)
    second = lax.slice_in_dim(value, HALF, 2 * HALF, axis=axis)
    return jnp.concatenate([second, first], axis=axis)


def kernel(cost_ref, bound_ref, start_ref, dual_ref, target_ref, owner_ref, local_ref,
           primal_ref, duals_ref, totals_ref,
           cost, bound, primal, owner, local, hot, own_half, ext, acc,
           packed, state, gath, part, rsz, deg_part, deg_z, deg_x, step, tot, tot_z, tot_x, back,
           sem_pack, sem_own, sem_loc, sem_cost, sem_bound, sem_primal, sem_agz, sem_rsz,
           sem_dz, sem_dx, sem_tz, sem_tx, sem_back, sem_dual):
    edges = cost_ref.shape[1]
    slots = ITERS * CHUNKS
    me = lax.axis_index("edge")
    my_x = lax.rem(me, X)
    my_z = lax.div(me, X)
    lane = lax.broadcasted_iota(jnp.int32, (GROUP, LANES), 1)
    upper = lax.broadcasted_iota(jnp.int32, (GROUP, LANES), 0) < HALF

    def x_of(j):
        return lax.rem(my_x + j, X)

    def at_x(j):
        return my_z * X + x_of(j)

    def at_z(j):
        return lax.rem(my_z + j, Z) * X + my_x

    def group(x):
        return pl.ds(pl.multiple_of(x * GROUP, GROUP), GROUP)

    def remote(src, dst, send, recv, device):
        return pltpu.make_async_remote_copy(
            src_ref=src, dst_ref=dst, send_sem=send, recv_sem=recv,
            device_id={"edge": device}, device_id_type=pl.DeviceIdType.MESH)

    def give(src, dst, sems, j):
        return remote(src, dst.at[X - j], sems.at[0, j], sems.at[1, X - j], at_x(j))

    def give_rows(src, dst, sems, j):
        return give(src.at[group(x_of(j))], dst, sems, j)

    def taken(dst, sems, j):
        return remote(dst.at[j], dst.at[j], sems.at[0, j], sems.at[1, j], at_x(j))

    def packs(j):
        return give(packed.at[x_of(j)], state, sem_pack, j)

    def agz(c):
        block = gath.at[c, my_z]
        return [remote(block, block, sem_agz.at[c, 0, j], sem_agz.at[c, 1, j], at_z(j)) for j in range(1, Z)]

    def to_z(c):
        return [remote(part.at[c, lax.rem(my_z + j, Z)], rsz.at[c, j - 1], sem_rsz.at[c, 0, j], sem_rsz.at[c, 1, j],
                       at_z(j)) for j in range(1, Z)]

    def deg_to_z():
        return [remote(deg_part.at[lax.rem(my_z + j, Z)], deg_z.at[j - 1], sem_dz.at[0, j], sem_dz.at[1, j], at_z(j))
                for j in range(1, Z)]

    def deg_to_x():
        return [give(deg_x.at[0], deg_x, sem_dx, j) for j in range(1, X)]

    def tot_to_z():
        return [remote(tot_z.at[my_z], tot_z.at[my_z], sem_tz.at[0, j], sem_tz.at[1, j], at_z(j))
                for j in range(1, Z)]

    def tot_to_x():
        return [remote(tot_x.at[my_x], tot_x.at[my_x], sem_tx.at[0, j], sem_tx.at[1, X - j], at_x(j))
                for j in range(1, X)]

    def primal_back(j):
        return remote(primal.at[j], primal_ref.at[group(my_x)], sem_back.at[0, j], sem_back.at[1, X - j], at_x(j))

    def dual_back(j):
        return remote(back.at[j], duals_ref.at[group(my_x)], sem_dual.at[0, j], sem_dual.at[1, X - j], at_x(j))

    def start(copies):
        for copy in copies:
            copy.start()

    def wait(copies):
        for copy in copies:
            copy.wait()

    for g in range(X):
        for kind, ref in enumerate((dual_ref, target_ref)):
            rows = ref[g * GROUP:(g + 1) * GROUP, :]
            low, high = rows[:, :LANES], rows[:, LANES:]
            packed[g, 2 * kind] = jnp.concatenate([low[:HALF], high[:HALF]], axis=0)
            packed[g, 2 * kind + 1] = jnp.concatenate([low[HALF:], high[HALF:]], axis=0)

    barrier = pltpu.get_barrier_semaphore()
    for j in range(1, Z):
        pl.semaphore_signal(barrier, inc=1, device_id={"edge": at_z(j)}, device_id_type=pl.DeviceIdType.MESH)
    for j in range(1, X):
        pl.semaphore_signal(barrier, inc=1, device_id={"edge": at_x(j)}, device_id_type=pl.DeviceIdType.MESH)
    pl.semaphore_wait(barrier, Z + X - 2)

    peers = (3, 1, 2)
    for j in peers:
        packs(j).start()
    for j in peers:
        give(owner_ref, owner, sem_own, j).start()
        give(local_ref, local, sem_loc, j).start()
    for j in peers:
        give_rows(cost_ref, cost, sem_cost, j).start()
        give_rows(bound_ref, bound, sem_bound, j).start()
        give_rows(start_ref, primal, sem_primal, j).start()

    state[0] = packed[my_x]
    owner[0] = owner_ref[...]
    local[0] = local_ref[...]
    cost[0] = cost_ref[group(my_x), :]
    bound[0] = bound_ref[group(my_x), :]
    primal[0] = start_ref[group(my_x), :]

    def build(j):
        second = lax.broadcasted_iota(jnp.int32, (2 * GROUP, 256), 0) >= GROUP

        def some(b, carry):
            here = pl.ds(pl.multiple_of(b * 256, 256), 256)
            cols = pl.ds(pl.multiple_of(j * edges + b * 256, 256), 256)
            for side in range(2):
                ids = local[j, side:side + 1, here]
                one = (lax.broadcasted_iota(jnp.int32, (256, 256), 0) == ids).astype(F32)
                hot[side, :, cols] = one.astype(BF16)
                names = jnp.broadcast_to(owner[j, side:side + 1, here], (2 * GROUP, 256))
                own_half[side, :, cols] = jnp.where(second, names - 1, names).astype(F32).astype(BF16)
            return carry

        lax.fori_loop(0, edges // 256, some, 0)

    build(0)
    for j in peers:
        packs(j).wait()
    for c in range(CHUNKS):
        for x in range(X):
            gath[c, my_z, x] = state[lax.rem(x + X - my_x, X), c]
        start(agz(c))

    degree = None
    for side in range(2):
        rows = lax.broadcasted_iota(jnp.int32, (OWNERS, edges), 0)
        named = (rows == owner_ref[side:side + 1, :]).astype(F32).astype(BF16)
        count = lax.dot_general(named, hot[side, :, :edges], (((1,), (1,)), ((), ())), preferred_element_type=F32)
        degree = count if degree is None else degree + count
    for z in range(Z):
        four = degree[z * X:(z + 1) * X]
        deg_part[z] = jnp.concatenate([four, four], axis=0)
    start(deg_to_z())
    tot[...] = jnp.zeros_like(tot)

    for j in peers:
        give(owner_ref, owner, sem_own, j).wait()
        give(local_ref, local, sem_loc, j).wait()

    def later(j, carry):
        build(j)
        return carry

    lax.fori_loop(1, X, later, 0)

    wait(deg_to_z())
    mine = deg_part[my_z]
    for j in range(Z - 1):
        mine = mine + deg_z[j]
    deg_x[0] = mine
    start(deg_to_x())

    def degree_done():
        wait(deg_to_x())
        whole = (deg_x[0] + deg_x[1]) + (deg_x[2] + deg_x[3])
        inverse = 1.0 / jnp.maximum(whole, 1.0)
        for x in range(X):
            low = jnp.broadcast_to(inverse[x:x + 1, :LANES], (GROUP, LANES))
            high = jnp.broadcast_to(inverse[x:x + 1, LANES:], (GROUP, LANES))
            step[x] = jnp.where(upper, low, high)

    def pull(t):
        c, sweep = lax.rem(t, CHUNKS), lax.div(t, CHUNKS)
        wait(agz(c))
        value = gath[c].reshape(OWNERS, GROUP, LANES)
        high = value.astype(BF16).astype(F32)
        low = value - high
        is_upper = lax.broadcasted_iota(jnp.int32, (OWNERS, GROUP, LANES), 1) < HALF
        first = jnp.where(is_upper, high, turn(low))
        second = jnp.where(is_upper, turn(high), low)
        left = jnp.concatenate([first, second], axis=2).reshape(OWNERS * GROUP, 2 * LANES).astype(BF16)
        in_upper = lax.broadcasted_iota(jnp.int32, (GROUP, edges), 0) < HALF
        in_chunk = (lax.broadcasted_iota(jnp.int32, (GROUP, edges), 0) >= HALF) == (c == 1)

        def block(j, spend):
            @pl.when((t == 0) & (j > 0))
            def _():
                taken(cost, sem_cost, j).wait_recv()
                taken(bound, sem_bound, j).wait_recv()
                taken(primal, sem_primal, j).wait_recv()

            cols = pl.ds(pl.multiple_of(j * edges, edges), edges)
            ends = []
            for side in range(2):
                all_rows = jnp.dot(left, hot[side, :, cols], preferred_element_type=F32)
                names = jnp.broadcast_to(owner[j, side:side + 1, :], (GROUP, edges))
                found = jnp.zeros((GROUP, edges), F32)
                for o in range(OWNERS):
                    found = jnp.where(names == o, all_rows[o * GROUP:(o + 1) * GROUP], found)
                ends.append(found)
            pulled = ends[0] - ends[1]
            pulled = pulled + turn(pulled)
            price, before = cost[j], primal[j]
            moved = jnp.minimum(jnp.maximum(before - 0.5 * (price - pulled), 0.0), bound[j])
            primal[j] = jnp.where(in_chunk, moved, before)
            extended = jnp.where(in_chunk, 2.0 * moved - before, 0.0)
            extended = extended + turn(extended)
            high = extended.astype(BF16).astype(F32)
            both = jnp.where(in_upper, high, extended - high)
            both = jnp.concatenate([both, both], axis=0).astype(BF16)
            ext[0, :, cols] = both
            ext[1, :, cols] = -both

            @pl.when((t == slots - 1) & (j > 0))
            def _():
                primal_back(j).start()

            return spend + jnp.sum(jnp.where(in_chunk, price * moved, 0.0), axis=1, keepdims=True)

        spend = lax.fori_loop(0, X, block, jnp.zeros((GROUP, 1), F32))
        tot[...] += jnp.where(lane == ITERS + sweep, jnp.broadcast_to(spend, (GROUP, LANES)), 0.0)

    def push(t):
        c = lax.rem(t, CHUNKS)
        acc[...] = jnp.zeros_like(acc)

        def block(j, carry):
            cols = pl.ds(pl.multiple_of(j * edges, edges), edges)
            for side in range(2):
                value, names = ext[side, :, cols], own_half[side, :, cols]
                zero = jnp.zeros_like(value)
                left = jnp.concatenate(
                    [jnp.where(names == BF16(o), value, zero) for o in range(0, OWNERS, 2)], axis=0)
                acc[...] += lax.dot_general(left, hot[side, :, cols], (((1,), (1,)), ((), ())),
                                            preferred_element_type=F32)
            return carry

        lax.fori_loop(0, X, block, 0)
        value = acc[...].reshape(OWNERS, GROUP, 2 * LANES)
        value = value + turn(value)
        is_upper = lax.broadcasted_iota(jnp.int32, (OWNERS, GROUP, LANES), 1) < HALF
        part[c] = jnp.where(is_upper, value[:, :, :LANES], value[:, :, LANES:]).reshape(Z, X, GROUP, LANES)
        start(to_z(c))

    def settle(t):
        c, sweep = lax.rem(t, CHUNKS), lax.div(t, CHUNKS)
        wait(to_z(c))
        squares = jnp.zeros((GROUP, LANES), F32)
        for x in range(X):
            place = lax.rem(x + X - my_x, X)
            applied = part[c, my_z, x]
            for j in range(Z - 1):
                applied = applied + rsz[c, j, x]
            residual = state[place, CHUNKS + c] - applied
            duals = state[place, c] + step[x] * residual
            state[place, c] = duals
            gath[c, my_z, x] = duals
            squares = squares + residual * residual
        square = jnp.broadcast_to(jnp.sum(squares, axis=1, keepdims=True), (GROUP, LANES))
        square = square + turn(square)
        tot[...] += jnp.where((lane == sweep) & (upper == (c == 0)), square, 0.0)

        @pl.when(sweep < ITERS - 1)
        def _():
            start(agz(c))

    def slot(t, carry):
        pull(t)

        @pl.when(t == 1)
        def _():
            degree_done()

        @pl.when(t >= 1)
        def _():
            settle(t - 1)

        push(t)
        return carry

    lax.fori_loop(0, slots, slot, 0)
    settle(slots - 1)

    tot_z[my_z] = tot[...]
    start(tot_to_z())
    for j in range(X):
        first, second = state[j, 0], state[j, 1]
        back[j] = jnp.concatenate(
            [jnp.concatenate([first[:HALF], second[:HALF]], axis=0),
             jnp.concatenate([first[HALF:], second[HALF:]], axis=0)], axis=1)
    for j in peers:
        dual_back(j).start()
    duals_ref[group(my_x), :] = back[0]
    primal_ref[group(my_x), :] = primal[0]
    for j in peers:
        give_rows(cost_ref, cost, sem_cost, j).wait_send()
        give_rows(bound_ref, bound, sem_bound, j).wait_send()
        give_rows(start_ref, primal, sem_primal, j).wait_send()
    wait(tot_to_z())
    mine = tot_z[0]
    for z in range(1, Z):
        mine = mine + tot_z[z]
    tot_x[my_x] = mine
    start(tot_to_x())
    wait([primal_back(j) for j in peers])
    wait([dual_back(j) for j in peers])
    wait(tot_to_x())
    every = jnp.concatenate([tot_x[x] for x in range(X)] + [jnp.zeros((LANES - X * GROUP, LANES), F32)], axis=0).T
    for i in range(ITERS):
        totals_ref[i, 0:1, :] = every[i:i + 1, :X * GROUP]
        totals_ref[i, 1:2, :] = every[ITERS + i:ITERS + i + 1, :X * GROUP]


def body(unit_cost, upper_bound, start_primal, start_dual, net_target, owners, local_ids):
    buckets, edges = unit_cost.shape
    accounts = start_dual.shape[1]
    tile = (GROUP, LANES)
    dma = pltpu.SemaphoreType.DMA
    vmem = pltpu.VMEM
    primal, duals, totals = pl.pallas_call(
        kernel,
        out_shape=(
            jax.ShapeDtypeStruct((buckets, edges), F32),
            jax.ShapeDtypeStruct((buckets, accounts), F32),
            jax.ShapeDtypeStruct((ITERS, 2, buckets), F32),
        ),
        in_specs=[pl.BlockSpec(memory_space=vmem)] * 7,
        out_specs=[pl.BlockSpec(memory_space=vmem)] * 3,
        scratch_shapes=[
            vmem((X, GROUP, edges), F32),
            vmem((X, GROUP, edges), F32),
            vmem((X, GROUP, edges), F32),
            vmem((X, 2, edges), jnp.int32),
            vmem((X, 2, edges), jnp.int32),
            vmem((2, accounts, X * edges), BF16),
            vmem((2, 2 * GROUP, X * edges), BF16),
            vmem((2, 2 * GROUP, X * edges), BF16),
            vmem((OWNERS * GROUP, accounts), F32),
            vmem((X, 2 * CHUNKS) + tile, F32),
            vmem((X, 2 * CHUNKS) + tile, F32),
            vmem((CHUNKS, Z, X) + tile, F32),
            vmem((CHUNKS, Z, X) + tile, F32),
            vmem((CHUNKS, Z - 1, X) + tile, F32),
            vmem((Z, GROUP, accounts), F32),
            vmem((Z - 1, GROUP, accounts), F32),
            vmem((X, GROUP, accounts), F32),
            vmem((X,) + tile, F32),
            vmem(tile, F32),
            vmem((Z,) + tile, F32),
            vmem((X,) + tile, F32),
            vmem((X, GROUP, accounts), F32),
            dma((2, X)),
            dma((2, X)),
            dma((2, X)),
            dma((2, X)),
            dma((2, X)),
            dma((2, X)),
            dma((CHUNKS, 2, Z)),
            dma((CHUNKS, 2, Z)),
            dma((2, Z)),
            dma((2, X)),
            dma((2, Z)),
            dma((2, X)),
            dma((2, X)),
            dma((2, X)),
        ],
        compiler_params=pltpu.CompilerParams(
            collective_id=0, has_side_effects=True, vmem_limit_bytes=58 * 2**20),
        cost_estimate=pl.CostEstimate(flops=52 * 10**9, bytes_accessed=4 * 2**20, transcendentals=0),
    )(unit_cost, upper_bound, start_primal, start_dual, net_target, owners.T, local_ids.T)
    return primal, duals, totals.transpose(1, 0, 2)


def solution(mesh):
    return jax.shard_map(
        body,
        mesh=mesh,
        in_specs=(
            P("bucket", "edge"),
            P("bucket", "edge"),
            P("bucket", "edge"),
            P("bucket", "edge"),
            P("bucket", "edge"),
            P("edge", None),
            P("edge", None),
        ),
        out_specs=(P("bucket", "edge"), P("bucket", "edge"), P(None, None, "bucket")),
        check_vma=False,
    )
```

```python
import jax
import jax.numpy as jnp
from jax import lax
from jax.experimental import pallas as pl
from jax.experimental.pallas import tpu as pltpu
from jax.sharding import PartitionSpec as P

ITERS = 3
X = 4
Z = 8
OWNERS = X * Z
FAR = (4, 3, 5, 2, 6, 1, 7)
HALF = 4
CHUNKS = 2
GROUP = HALF * CHUNKS
LANES = 128
F32 = jnp.float32
BF16 = jnp.bfloat16


def turn(value):
    axis = value.ndim - 2
    first = lax.slice_in_dim(value, 0, HALF, axis=axis)
    second = lax.slice_in_dim(value, HALF, 2 * HALF, axis=axis)
    return jnp.concatenate([second, first], axis=axis)


def kernel(cost_ref, bound_ref, start_ref, dual_ref, target_ref, owner_ref, local_ref,
           primal_ref, duals_ref, totals_ref,
           cost, bound, primal, owner, local, hot, own_half, ext, left, acc,
           packed, state, gath, part, rsz, deg_part, deg_z, deg_x, step, tot, tot_z, tot_x, back,
           sem_pack, sem_own, sem_loc, sem_cost, sem_bound, sem_primal, sem_agz, sem_rsz,
           sem_dz, sem_dx, sem_tz, sem_tx, sem_back, sem_dual):
    edges = cost_ref.shape[1]
    slots = ITERS * CHUNKS
    me = lax.axis_index("edge")
    my_x = lax.rem(me, X)
    my_z = lax.div(me, X)
    lane = lax.broadcasted_iota(jnp.int32, (GROUP, LANES), 1)
    upper = lax.broadcasted_iota(jnp.int32, (GROUP, LANES), 0) < HALF

    def x_of(j):
        return lax.rem(my_x + j, X)

    def at_x(j):
        return my_z * X + x_of(j)

    def at_z(j):
        return lax.rem(my_z + j, Z) * X + my_x

    def group(x):
        return pl.ds(pl.multiple_of(x * GROUP, GROUP), GROUP)

    def remote(src, dst, send, recv, device):
        return pltpu.make_async_remote_copy(
            src_ref=src, dst_ref=dst, send_sem=send, recv_sem=recv,
            device_id={"edge": device}, device_id_type=pl.DeviceIdType.MESH)

    def give(src, dst, sems, j):
        return remote(src, dst.at[X - j], sems.at[0, j], sems.at[1, X - j], at_x(j))

    def give_rows(src, dst, sems, j):
        return give(src.at[group(x_of(j))], dst, sems, j)

    def taken(dst, sems, j):
        return remote(dst.at[j], dst.at[j], sems.at[0, j], sems.at[1, j], at_x(j))

    def packs(j):
        return give(packed.at[x_of(j)], state, sem_pack, j)

    def agz(c):
        block = gath.at[c, my_z]
        return [remote(block, block, sem_agz.at[c, 0, j], sem_agz.at[c, 1, j], at_z(j)) for j in FAR]

    def to_z(c):
        return [remote(part.at[c, lax.rem(my_z + j, Z)], rsz.at[c, j - 1], sem_rsz.at[c, 0, j], sem_rsz.at[c, 1, j],
                       at_z(j)) for j in FAR]

    def deg_to_z():
        return [remote(deg_part.at[lax.rem(my_z + j, Z)], deg_z.at[j - 1], sem_dz.at[0, j], sem_dz.at[1, j], at_z(j))
                for j in range(1, Z)]

    def deg_to_x():
        return [give(deg_x.at[0], deg_x, sem_dx, j) for j in range(1, X)]

    def tot_to_z():
        return [remote(tot_z.at[my_z], tot_z.at[my_z], sem_tz.at[0, j], sem_tz.at[1, j], at_z(j))
                for j in range(1, Z)]

    def tot_to_x():
        return [remote(tot_x.at[my_x], tot_x.at[my_x], sem_tx.at[0, j], sem_tx.at[1, X - j], at_x(j))
                for j in range(1, X)]

    def primal_back(j):
        return remote(primal.at[j], primal_ref.at[group(my_x)], sem_back.at[0, j], sem_back.at[1, X - j], at_x(j))

    def dual_back(j):
        return remote(back.at[j], duals_ref.at[group(my_x)], sem_dual.at[0, j], sem_dual.at[1, X - j], at_x(j))

    def start(copies):
        for copy in copies:
            copy.start()

    def wait(copies):
        for copy in copies:
            copy.wait()

    for g in range(X):
        for kind, ref in enumerate((dual_ref, target_ref)):
            rows = ref[g * GROUP:(g + 1) * GROUP, :]
            low, high = rows[:, :LANES], rows[:, LANES:]
            packed[g, 2 * kind] = jnp.concatenate([low[:HALF], high[:HALF]], axis=0)
            packed[g, 2 * kind + 1] = jnp.concatenate([low[HALF:], high[HALF:]], axis=0)

    barrier = pltpu.get_barrier_semaphore()
    for j in range(1, Z):
        pl.semaphore_signal(barrier, inc=1, device_id={"edge": at_z(j)}, device_id_type=pl.DeviceIdType.MESH)
    for j in range(1, X):
        pl.semaphore_signal(barrier, inc=1, device_id={"edge": at_x(j)}, device_id_type=pl.DeviceIdType.MESH)
    pl.semaphore_wait(barrier, Z + X - 2)

    peers = (3, 1, 2)

    def give_arrays(j):
        return [give_rows(cost_ref, cost, sem_cost, j), give_rows(bound_ref, bound, sem_bound, j),
                give_rows(start_ref, primal, sem_primal, j)]

    for j in peers:
        packs(j).start()
    for j in peers:
        give(owner_ref, owner, sem_own, j).start()
        give(local_ref, local, sem_loc, j).start()

    state[0] = packed[my_x]
    owner[0] = owner_ref[...]
    local[0] = local_ref[...]
    cost[0] = cost_ref[group(my_x), :]
    bound[0] = bound_ref[group(my_x), :]
    primal[0] = start_ref[group(my_x), :]

    def build(j):
        second = lax.broadcasted_iota(jnp.int32, (2 * GROUP, 256), 0) >= GROUP

        def some(b, carry):
            here = pl.ds(pl.multiple_of(b * 256, 256), 256)
            cols = pl.ds(pl.multiple_of(j * edges + b * 256, 256), 256)
            for side in range(2):
                ids = local[j, side:side + 1, here]
                one = (lax.broadcasted_iota(jnp.int32, (256, 256), 0) == ids).astype(F32)
                hot[side, :, cols] = one.astype(BF16)
                names = jnp.broadcast_to(owner[j, side:side + 1, here], (2 * GROUP, 256))
                own_half[side, :, cols] = jnp.where(second, names - 1, names).astype(F32).astype(BF16)
            return carry

        lax.fori_loop(0, edges // 256, some, 0)

    for j in peers:
        packs(j).wait()
    for c in range(CHUNKS):
        for x in range(X):
            gath[c, my_z, x] = state[lax.rem(x + X - my_x, X), c]
        start(agz(c))
    start(give_arrays(3) + give_arrays(1))
    build(0)

    degree = None
    for side in range(2):
        rows = lax.broadcasted_iota(jnp.int32, (OWNERS, edges), 0)
        named = (rows == owner_ref[side:side + 1, :]).astype(F32).astype(BF16)
        count = lax.dot_general(named, hot[side, :, :edges], (((1,), (1,)), ((), ())), preferred_element_type=F32)
        degree = count if degree is None else degree + count
    for z in range(Z):
        four = degree[z * X:(z + 1) * X]
        deg_part[z] = jnp.concatenate([four, four], axis=0)
    start(deg_to_z())
    tot[...] = jnp.zeros_like(tot)

    for j in peers:
        give(owner_ref, owner, sem_own, j).wait()
        give(local_ref, local, sem_loc, j).wait()
    start(give_arrays(2))

    def later(j, carry):
        build(j)
        return carry

    lax.fori_loop(1, X, later, 0)

    wait(deg_to_z())
    mine = deg_part[my_z]
    for j in range(Z - 1):
        mine = mine + deg_z[j]
    deg_x[0] = mine
    start(deg_to_x())

    def degree_done():
        wait(deg_to_x())
        whole = (deg_x[0] + deg_x[1]) + (deg_x[2] + deg_x[3])
        inverse = 1.0 / jnp.maximum(whole, 1.0)
        for x in range(X):
            low = jnp.broadcast_to(inverse[x:x + 1, :LANES], (GROUP, LANES))
            high = jnp.broadcast_to(inverse[x:x + 1, LANES:], (GROUP, LANES))
            step[x] = jnp.where(upper, low, high)

    def settle(t):
        c, sweep = lax.rem(t, CHUNKS), lax.div(t, CHUNKS)
        wait(to_z(c))
        squares = jnp.zeros((GROUP, LANES), F32)
        for x in range(X):
            place = lax.rem(x + X - my_x, X)
            applied = part[c, my_z, x]
            for j in range(Z - 1):
                applied = applied + rsz[c, j, x]
            residual = state[place, CHUNKS + c] - applied
            duals = state[place, c] + step[x] * residual
            state[place, c] = duals
            gath[c, my_z, x] = duals
            squares = squares + residual * residual
        square = jnp.broadcast_to(jnp.sum(squares, axis=1, keepdims=True), (GROUP, LANES))
        square = square + turn(square)
        tot[...] += jnp.where((lane == sweep) & (upper == (c == 0)), square, 0.0)

        @pl.when(sweep < ITERS - 1)
        def _():
            start(agz(c))

    def slot(t, carry):
        c, sweep = lax.rem(t, CHUNKS), lax.div(t, CHUNKS)
        wait(agz(c))
        value = gath[c].reshape(OWNERS, GROUP, LANES)
        high = value.astype(BF16).astype(F32)
        low = value - high
        is_upper = lax.broadcasted_iota(jnp.int32, (OWNERS, GROUP, LANES), 1) < HALF
        first = jnp.where(is_upper, high, turn(low))
        second = jnp.where(is_upper, turn(high), low)
        left[...] = jnp.concatenate([first, second], axis=2).reshape(OWNERS * GROUP, 2 * LANES).astype(BF16)
        in_upper = lax.broadcasted_iota(jnp.int32, (GROUP, edges), 0) < HALF
        in_chunk = (lax.broadcasted_iota(jnp.int32, (GROUP, edges), 0) >= HALF) == (c == 1)
        acc[...] = jnp.zeros_like(acc)

        def block(i, spend):
            j = jnp.where(i < 2, i, 5 - i)

            @pl.when((t == 0) & (i > 0))
            def _():
                taken(cost, sem_cost, j).wait_recv()
                taken(bound, sem_bound, j).wait_recv()
                taken(primal, sem_primal, j).wait_recv()

            @pl.when((t == 1) & (i == 2))
            def _():
                degree_done()

            @pl.when((t >= 1) & (i == 2))
            def _():
                settle(t - 1)

            cols = pl.ds(pl.multiple_of(j * edges, edges), edges)
            ends = []
            for side in range(2):
                all_rows = jnp.dot(left[...], hot[side, :, cols], preferred_element_type=F32)
                names = jnp.broadcast_to(owner[j, side:side + 1, :], (GROUP, edges))
                found = jnp.zeros((GROUP, edges), F32)
                for o in range(OWNERS):
                    found = jnp.where(names == o, all_rows[o * GROUP:(o + 1) * GROUP], found)
                ends.append(found)
            pulled = ends[0] - ends[1]
            pulled = pulled + turn(pulled)
            price, before = cost[j], primal[j]
            moved = jnp.minimum(jnp.maximum(before - 0.5 * (price - pulled), 0.0), bound[j])
            primal[j] = jnp.where(in_chunk, moved, before)
            extended = jnp.where(in_chunk, 2.0 * moved - before, 0.0)
            extended = extended + turn(extended)
            high = extended.astype(BF16).astype(F32)
            both = jnp.where(in_upper, high, extended - high)
            both = jnp.concatenate([both, both], axis=0).astype(BF16)
            ext[0] = both
            ext[1] = -both

            @pl.when((t == slots - 1) & (i > 0))
            def _():
                primal_back(j).start()

            for side in range(2):
                value, names = ext[side], own_half[side, :, cols]
                zero = jnp.zeros_like(value)
                masked = jnp.concatenate(
                    [jnp.where(names == BF16(o), value, zero) for o in range(0, OWNERS, 2)], axis=0)
                acc[...] += lax.dot_general(masked, hot[side, :, cols], (((1,), (1,)), ((), ())),
                                            preferred_element_type=F32)
            return spend + jnp.sum(jnp.where(in_chunk, price * moved, 0.0), axis=1, keepdims=True)

        spend = lax.fori_loop(0, X, block, jnp.zeros((GROUP, 1), F32))
        tot[...] += jnp.where(lane == ITERS + sweep, jnp.broadcast_to(spend, (GROUP, LANES)), 0.0)
        value = acc[...].reshape(OWNERS, GROUP, 2 * LANES)
        value = value + turn(value)
        part[c] = jnp.where(is_upper, value[:, :, :LANES], value[:, :, LANES:]).reshape(Z, X, GROUP, LANES)
        start(to_z(c))
        return carry

    lax.fori_loop(0, slots, slot, 0)
    settle(slots - 1)

    tot_z[my_z] = tot[...]
    start(tot_to_z())
    for j in range(X):
        first, second = state[j, 0], state[j, 1]
        back[j] = jnp.concatenate(
            [jnp.concatenate([first[:HALF], second[:HALF]], axis=0),
             jnp.concatenate([first[HALF:], second[HALF:]], axis=0)], axis=1)
    for j in peers:
        dual_back(j).start()
    duals_ref[group(my_x), :] = back[0]
    primal_ref[group(my_x), :] = primal[0]
    for j in peers:
        for copy in give_arrays(j):
            copy.wait_send()
    wait(tot_to_z())
    mine = tot_z[0]
    for z in range(1, Z):
        mine = mine + tot_z[z]
    tot_x[my_x] = mine
    start(tot_to_x())
    wait([primal_back(j) for j in peers])
    wait([dual_back(j) for j in peers])
    wait(tot_to_x())
    every = jnp.concatenate([tot_x[x] for x in range(X)] + [jnp.zeros((LANES - X * GROUP, LANES), F32)], axis=0).T
    for i in range(ITERS):
        totals_ref[i, 0:1, :] = every[i:i + 1, :X * GROUP]
        totals_ref[i, 1:2, :] = every[ITERS + i:ITERS + i + 1, :X * GROUP]


def finish(*refs):
    count = len(refs) // 2
    sems = refs[-1]
    copies = [pltpu.make_async_copy(refs[i], refs[count + i], sems.at[i]) for i in range(count)]
    for copy in copies:
        copy.start()
    for copy in copies:
        copy.wait()


def body(unit_cost, upper_bound, start_primal, start_dual, net_target, owners, local_ids):
    buckets, edges = unit_cost.shape
    accounts = start_dual.shape[1]
    tile = (GROUP, LANES)
    dma = pltpu.SemaphoreType.DMA
    vmem = pltpu.VMEM
    primal, duals, totals = pl.pallas_call(
        kernel,
        out_shape=(
            jax.ShapeDtypeStruct((buckets, edges), F32),
            jax.ShapeDtypeStruct((buckets, accounts), F32),
            jax.ShapeDtypeStruct((ITERS, 2, buckets), F32),
        ),
        in_specs=[pl.BlockSpec(memory_space=vmem)] * 7,
        out_specs=[pl.BlockSpec(memory_space=vmem)] * 3,
        scratch_shapes=[
            vmem((X, GROUP, edges), F32),
            vmem((X, GROUP, edges), F32),
            vmem((X, GROUP, edges), F32),
            vmem((X, 2, edges), jnp.int32),
            vmem((X, 2, edges), jnp.int32),
            vmem((2, accounts, X * edges), BF16),
            vmem((2, 2 * GROUP, X * edges), BF16),
            vmem((2, 2 * GROUP, edges), BF16),
            vmem((OWNERS * GROUP, accounts), BF16),
            vmem((OWNERS * GROUP, accounts), F32),
            vmem((X, 2 * CHUNKS) + tile, F32),
            vmem((X, 2 * CHUNKS) + tile, F32),
            vmem((CHUNKS, Z, X) + tile, F32),
            vmem((CHUNKS, Z, X) + tile, F32),
            vmem((CHUNKS, Z - 1, X) + tile, F32),
            vmem((Z, GROUP, accounts), F32),
            vmem((Z - 1, GROUP, accounts), F32),
            vmem((X, GROUP, accounts), F32),
            vmem((X,) + tile, F32),
            vmem(tile, F32),
            vmem((Z,) + tile, F32),
            vmem((X,) + tile, F32),
            vmem((X, GROUP, accounts), F32),
            dma((2, X)),
            dma((2, X)),
            dma((2, X)),
            dma((2, X)),
            dma((2, X)),
            dma((2, X)),
            dma((CHUNKS, 2, Z)),
            dma((CHUNKS, 2, Z)),
            dma((2, Z)),
            dma((2, X)),
            dma((2, Z)),
            dma((2, X)),
            dma((2, X)),
            dma((2, X)),
        ],
        compiler_params=pltpu.CompilerParams(
            collective_id=0, has_side_effects=True, vmem_limit_bytes=58 * 2**20),
        cost_estimate=pl.CostEstimate(flops=52 * 10**9, bytes_accessed=4 * 2**20, transcendentals=0),
    )(unit_cost, upper_bound, start_primal, start_dual, net_target, owners.T, local_ids.T)
    results = (primal, duals, totals)
    primal, duals, totals = pl.pallas_call(
        finish,
        out_shape=tuple(jax.ShapeDtypeStruct(r.shape, r.dtype) for r in results),
        in_specs=[pl.BlockSpec(memory_space=pl.ANY)] * 3,
        out_specs=[pl.BlockSpec(memory_space=pl.ANY)] * 3,
        scratch_shapes=[dma((3,))],
        compiler_params=pltpu.CompilerParams(vmem_limit_bytes=60 * 2**20),
    )(*results)
    return primal, duals, totals.transpose(1, 0, 2)


def solution(mesh):
    return jax.shard_map(
        body,
        mesh=mesh,
        in_specs=(
            P("bucket", "edge"),
            P("bucket", "edge"),
            P("bucket", "edge"),
            P("bucket", "edge"),
            P("bucket", "edge"),
            P("edge", None),
            P("edge", None),
        ),
        out_specs=(P("bucket", "edge"), P("bucket", "edge"), P(None, None, "bucket")),
        check_vma=False,
    )
```

```python
import jax
import jax.numpy as jnp
from jax import lax
from jax.experimental import pallas as pl
from jax.experimental.pallas import tpu as pltpu
from jax.sharding import PartitionSpec as P

ITERS = 3
X = 4
Z = 8
OWNERS = X * Z
FAR = (4, 3, 5, 2, 6, 1, 7)
HALF = 4
CHUNKS = 2
GROUP = HALF * CHUNKS
LANES = 128
F32 = jnp.float32
BF16 = jnp.bfloat16


def turn(value):
    axis = value.ndim - 2
    first = lax.slice_in_dim(value, 0, HALF, axis=axis)
    second = lax.slice_in_dim(value, HALF, 2 * HALF, axis=axis)
    return jnp.concatenate([second, first], axis=axis)


def kernel(cost_ref, bound_ref, start_ref, dual_ref, target_ref, owner_ref, local_ref,
           primal_ref, duals_ref, totals_ref,
           cost, bound, primal, owner, local, hot, own_half, ext, left, acc,
           packed, state, gath, part, rsz, deg_part, deg_z, deg_x, step, tot, tot_all, back,
           sem_pack, sem_own, sem_loc, sem_cost, sem_bound, sem_primal, sem_agz, sem_rsz,
           sem_dz, sem_dx, sem_tot, sem_back, sem_dual):
    edges = cost_ref.shape[1]
    slots = ITERS * CHUNKS
    me = lax.axis_index("edge")
    my_x = lax.rem(me, X)
    my_z = lax.div(me, X)
    kind = lax.broadcasted_iota(jnp.int32, (GROUP, LANES), 1) >> 5
    upper = lax.broadcasted_iota(jnp.int32, (GROUP, LANES), 0) < HALF

    def x_of(j):
        return lax.rem(my_x + j, X)

    def at_x(j):
        return my_z * X + x_of(j)

    def at_z(j):
        return lax.rem(my_z + j, Z) * X + my_x

    def group(x):
        return pl.ds(pl.multiple_of(x * GROUP, GROUP), GROUP)

    def remote(src, dst, send, recv, device):
        return pltpu.make_async_remote_copy(
            src_ref=src, dst_ref=dst, send_sem=send, recv_sem=recv,
            device_id={"edge": device}, device_id_type=pl.DeviceIdType.MESH)

    def give(src, dst, sems, j):
        return remote(src, dst.at[X - j], sems.at[0, j], sems.at[1, X - j], at_x(j))

    def give_rows(src, dst, sems, j):
        return give(src.at[group(x_of(j))], dst, sems, j)

    def taken(dst, sems, j):
        return remote(dst.at[j], dst.at[j], sems.at[0, j], sems.at[1, j], at_x(j))

    def packs(j):
        return give(packed.at[x_of(j)], state, sem_pack, j)

    def agz(c):
        block = gath.at[c, my_z]
        return [remote(block, block, sem_agz.at[c, 0], sem_agz.at[c, 1], at_z(j)) for j in FAR]

    def agz_all(c):
        blocks = gath.at[c, pl.ds(0, Z - 1)]
        return [remote(blocks, blocks, sem_agz.at[c, 0], sem_agz.at[c, 1], at_z(1))]

    def to_z(c):
        return [remote(part.at[c, lax.rem(my_z + j, Z)], rsz.at[c, j - 1], sem_rsz.at[c, 0], sem_rsz.at[c, 1], at_z(j))
                for j in FAR]

    def to_z_all(c):
        return [remote(part.at[c, pl.ds(0, Z - 1)], rsz.at[c], sem_rsz.at[c, 0], sem_rsz.at[c, 1], at_z(1))]

    def deg_to_z():
        return [remote(deg_part.at[lax.rem(my_z + j, Z)], deg_z.at[j - 1], sem_dz.at[0, j], sem_dz.at[1, j], at_z(j))
                for j in range(1, Z)]

    def deg_to_x():
        return [give(deg_x.at[0], deg_x, sem_dx, j) for j in range(1, X)]

    def tot_out(j):
        mine = tot_all.at[me]
        return remote(mine, mine, sem_tot.at[0], sem_tot.at[1], lax.rem(me + j, OWNERS))

    def tot_in():
        rows = tot_all.at[pl.ds(0, OWNERS - 1)]
        return remote(rows, rows, sem_tot.at[0], sem_tot.at[1], at_z(1))

    def primal_back(j):
        return remote(primal.at[j], primal_ref.at[group(my_x)], sem_back.at[0, j], sem_back.at[1, X - j], at_x(j))

    def dual_back(j):
        return remote(back.at[j], duals_ref.at[group(my_x)], sem_dual.at[0, j], sem_dual.at[1, X - j], at_x(j))

    def start(copies):
        for copy in copies:
            copy.start()

    def wait(copies):
        for copy in copies:
            copy.wait()

    for g in range(X):
        for which, ref in enumerate((dual_ref, target_ref)):
            rows = ref[g * GROUP:(g + 1) * GROUP, :]
            low, high = rows[:, :LANES], rows[:, LANES:]
            packed[g, 2 * which] = jnp.concatenate([low[:HALF], high[:HALF]], axis=0)
            packed[g, 2 * which + 1] = jnp.concatenate([low[HALF:], high[HALF:]], axis=0)

    barrier = pltpu.get_barrier_semaphore()
    for j in range(1, OWNERS):
        pl.semaphore_signal(barrier, inc=1, device_id={"edge": lax.rem(me + j, OWNERS)},
                            device_id_type=pl.DeviceIdType.MESH)
    pl.semaphore_wait(barrier, OWNERS - 1)

    peers = (3, 1, 2)

    def give_arrays(j):
        return [give_rows(cost_ref, cost, sem_cost, j), give_rows(bound_ref, bound, sem_bound, j),
                give_rows(start_ref, primal, sem_primal, j)]

    for j in peers:
        packs(j).start()
    for j in peers:
        give(owner_ref, owner, sem_own, j).start()
        give(local_ref, local, sem_loc, j).start()

    state[0] = packed[my_x]
    owner[0] = owner_ref[...]
    local[0] = local_ref[...]
    cost[0] = cost_ref[group(my_x), :]
    bound[0] = bound_ref[group(my_x), :]
    primal[0] = start_ref[group(my_x), :]

    def build(j):
        second = lax.broadcasted_iota(jnp.int32, (2 * GROUP, 256), 0) >= GROUP

        def some(b, carry):
            here = pl.ds(pl.multiple_of(b * 256, 256), 256)
            cols = pl.ds(pl.multiple_of(j * edges + b * 256, 256), 256)
            for side in range(2):
                ids = local[j, side:side + 1, here]
                one = (lax.broadcasted_iota(jnp.int32, (256, 256), 0) == ids).astype(F32)
                hot[side, :, cols] = one.astype(BF16)
                names = jnp.broadcast_to(owner[j, side:side + 1, here], (2 * GROUP, 256))
                own_half[side, :, cols] = jnp.where(second, names - 1, names).astype(F32).astype(BF16)
            return carry

        lax.fori_loop(0, edges // 256, some, 0)

    for j in peers:
        packs(j).wait()
    for c in range(CHUNKS):
        for x in range(X):
            gath[c, my_z, x] = state[lax.rem(x + X - my_x, X), c]
        start(agz(c))
    start(give_arrays(3) + give_arrays(1))
    build(0)

    degree = None
    for side in range(2):
        rows = lax.broadcasted_iota(jnp.int32, (OWNERS, edges), 0)
        named = (rows == owner_ref[side:side + 1, :]).astype(F32).astype(BF16)
        count = lax.dot_general(named, hot[side, :, :edges], (((1,), (1,)), ((), ())), preferred_element_type=F32)
        degree = count if degree is None else degree + count
    for z in range(Z):
        four = degree[z * X:(z + 1) * X]
        deg_part[z] = jnp.concatenate([four, four], axis=0)
    start(deg_to_z())
    tot[...] = jnp.zeros_like(tot)

    for j in peers:
        give(owner_ref, owner, sem_own, j).wait()
        give(local_ref, local, sem_loc, j).wait()
    start(give_arrays(2))

    def later(j, carry):
        build(j)
        return carry

    lax.fori_loop(1, X, later, 0)

    wait(deg_to_z())
    mine = deg_part[my_z]
    for j in range(Z - 1):
        mine = mine + deg_z[j]
    deg_x[0] = mine
    start(deg_to_x())

    def degree_done():
        wait(deg_to_x())
        whole = (deg_x[0] + deg_x[1]) + (deg_x[2] + deg_x[3])
        inverse = 1.0 / jnp.maximum(whole, 1.0)
        for x in range(X):
            low = jnp.broadcast_to(inverse[x:x + 1, :LANES], (GROUP, LANES))
            high = jnp.broadcast_to(inverse[x:x + 1, LANES:], (GROUP, LANES))
            step[x] = jnp.where(upper, low, high)

    def settle(t):
        c, sweep = lax.rem(t, CHUNKS), lax.div(t, CHUNKS)
        wait(to_z_all(c))
        squares = jnp.zeros((GROUP, LANES), F32)
        for x in range(X):
            place = lax.rem(x + X - my_x, X)
            applied = part[c, my_z, x]
            for j in range(Z - 1):
                applied = applied + rsz[c, j, x]
            residual = state[place, CHUNKS + c] - applied
            duals = state[place, c] + step[x] * residual
            state[place, c] = duals
            gath[c, my_z, x] = duals
            squares = squares + residual * residual
        square = jnp.broadcast_to(jnp.sum(squares, axis=1, keepdims=True), (GROUP, LANES))
        square = square + turn(square)
        tot[0] += jnp.where((kind == sweep) & (upper == (c == 0)), square, 0.0)

        @pl.when(sweep < ITERS - 1)
        def _():
            start(agz(c))

    def slot(t, carry):
        c, sweep = lax.rem(t, CHUNKS), lax.div(t, CHUNKS)
        wait(agz_all(c))
        value = gath[c].reshape(OWNERS, GROUP, LANES)
        high = value.astype(BF16).astype(F32)
        low = value - high
        is_upper = lax.broadcasted_iota(jnp.int32, (OWNERS, GROUP, LANES), 1) < HALF
        first = jnp.where(is_upper, high, turn(low))
        second = jnp.where(is_upper, turn(high), low)
        left[...] = jnp.concatenate([first, second], axis=2).reshape(OWNERS * GROUP, 2 * LANES).astype(BF16)
        in_upper = lax.broadcasted_iota(jnp.int32, (GROUP, edges), 0) < HALF
        in_chunk = (lax.broadcasted_iota(jnp.int32, (GROUP, edges), 0) >= HALF) == (c == 1)
        acc[...] = jnp.zeros_like(acc)

        def place(i):
            return jnp.where(i < 2, i, 5 - i)

        def pull(i, carry):
            j = place(i)

            @pl.when((t == 0) & (i > 0))
            def _():
                taken(cost, sem_cost, j).wait_recv()
                taken(bound, sem_bound, j).wait_recv()
                taken(primal, sem_primal, j).wait_recv()

            cols = pl.ds(pl.multiple_of(j * edges, edges), edges)
            ends = []
            for side in range(2):
                all_rows = jnp.dot(left[...], hot[side, :, cols], preferred_element_type=F32)
                names = jnp.broadcast_to(owner[j, side:side + 1, :], (GROUP, edges))
                found = jnp.zeros((GROUP, edges), F32)
                for o in range(OWNERS):
                    found = jnp.where(names == o, all_rows[o * GROUP:(o + 1) * GROUP], found)
                ends.append(found)
            pulled = ends[0] - ends[1]
            pulled = pulled + turn(pulled)
            price, before = cost[j], primal[j]
            moved = jnp.minimum(jnp.maximum(before - 0.5 * (price - pulled), 0.0), bound[j])
            primal[j] = jnp.where(in_chunk, moved, before)
            extended = jnp.where(in_chunk, 2.0 * moved - before, 0.0)
            extended = extended + turn(extended)
            high = extended.astype(BF16).astype(F32)
            both = jnp.where(in_upper, high, extended - high)
            both = jnp.concatenate([both, both], axis=0).astype(BF16)
            ext[0, :, cols] = both
            ext[1, :, cols] = -both
            spend = jnp.sum(jnp.where(in_chunk, price * moved, 0.0), axis=1, keepdims=True)
            tot[1] += jnp.where(kind == sweep, jnp.broadcast_to(spend, (GROUP, LANES)), 0.0)

            @pl.when((t == slots - 1) & (i > 0))
            def _():
                primal_back(j).start()

            return carry

        def push(i, carry):
            j = place(i)
            cols = pl.ds(pl.multiple_of(j * edges, edges), edges)
            for side in range(2):
                value, names = ext[side, :, cols], own_half[side, :, cols]
                zero = jnp.zeros_like(value)
                masked = jnp.concatenate(
                    [jnp.where(names == BF16(o), value, zero) for o in range(0, OWNERS, 2)], axis=0)
                acc[...] += lax.dot_general(masked, hot[side, :, cols], (((1,), (1,)), ((), ())),
                                            preferred_element_type=F32)
            return carry

        def turns(p, carry):
            low, high = jnp.where(p == 0, 0, X - 1), jnp.where((t == 0) & (p == 0), X - 1, X)
            lax.fori_loop(low, high, pull, 0)

            @pl.when(t == 1)
            def _():
                degree_done()

            @pl.when(t >= 1)
            def _():
                settle(t - 1)

            lax.fori_loop(low, high, push, 0)
            return carry

        lax.fori_loop(0, jnp.where(t == 0, 2, 1), turns, 0)
        value = acc[...].reshape(OWNERS, GROUP, 2 * LANES)
        value = value + turn(value)
        part[c] = jnp.where(is_upper, value[:, :, :LANES], value[:, :, LANES:]).reshape(Z, X, GROUP, LANES)
        start(to_z(c))
        return carry

    lax.fori_loop(0, slots, slot, 0)
    settle(slots - 1)

    lane = lax.broadcasted_iota(jnp.int32, (GROUP, LANES), 1) & (X * GROUP - 1)
    bucket = lax.broadcasted_iota(jnp.int32, (GROUP, LANES), 0) + my_x * GROUP
    for side in range(2):
        row = jnp.sum(jnp.where(lane == bucket, tot[side], 0.0), axis=0, keepdims=True)
        tot_all[me, :, side * LANES:(side + 1) * LANES] = row
    for j in range(1, OWNERS):
        tot_out(j).start()
    for j in range(X):
        first, second = state[j, 0], state[j, 1]
        back[j] = jnp.concatenate(
            [jnp.concatenate([first[:HALF], second[:HALF]], axis=0),
             jnp.concatenate([first[HALF:], second[HALF:]], axis=0)], axis=1)
    for j in peers:
        dual_back(j).start()
    duals_ref[group(my_x), :] = back[0]
    primal_ref[group(my_x), :] = primal[0]
    for j in peers:
        for copy in give_arrays(j):
            copy.wait_send()
    wait([primal_back(j) for j in peers])
    wait([dual_back(j) for j in peers])
    tot_in().wait()
    total = tot_all[0]
    for other in range(1, OWNERS):
        total = total + tot_all[other]
    for side in range(2):
        row = jnp.broadcast_to(total[:, side * LANES:(side + 1) * LANES], (GROUP, LANES))
        for i in range(ITERS):
            turned = pltpu.roll(row, (LANES - i * X * GROUP) % LANES, 1)
            totals_ref[i, side:side + 1, :] = turned[:1, :X * GROUP]


def finish(*refs):
    count = len(refs) // 2
    for i in range(count):
        refs[count + i][...] = refs[i][...]


def body(unit_cost, upper_bound, start_primal, start_dual, net_target, owners, local_ids):
    buckets, edges = unit_cost.shape
    accounts = start_dual.shape[1]
    tile = (GROUP, LANES)
    dma = pltpu.SemaphoreType.DMA
    vmem = pltpu.VMEM
    primal, duals, totals = pl.pallas_call(
        kernel,
        out_shape=(
            jax.ShapeDtypeStruct((buckets, edges), F32),
            jax.ShapeDtypeStruct((buckets, accounts), F32),
            jax.ShapeDtypeStruct((ITERS, 2, buckets), F32),
        ),
        in_specs=[pl.BlockSpec(memory_space=vmem)] * 7,
        out_specs=[pl.BlockSpec(memory_space=vmem)] * 3,
        scratch_shapes=[
            vmem((X, GROUP, edges), F32),
            vmem((X, GROUP, edges), F32),
            vmem((X, GROUP, edges), F32),
            vmem((X, 2, edges), jnp.int32),
            vmem((X, 2, edges), jnp.int32),
            vmem((2, accounts, X * edges), BF16),
            vmem((2, 2 * GROUP, X * edges), BF16),
            vmem((2, 2 * GROUP, X * edges), BF16),
            vmem((OWNERS * GROUP, accounts), BF16),
            vmem((OWNERS * GROUP, accounts), F32),
            vmem((X, 2 * CHUNKS) + tile, F32),
            vmem((X, 2 * CHUNKS) + tile, F32),
            vmem((CHUNKS, Z, X) + tile, F32),
            vmem((CHUNKS, Z, X) + tile, F32),
            vmem((CHUNKS, Z - 1, X) + tile, F32),
            vmem((Z, GROUP, accounts), F32),
            vmem((Z - 1, GROUP, accounts), F32),
            vmem((X, GROUP, accounts), F32),
            vmem((X,) + tile, F32),
            vmem((2,) + tile, F32),
            vmem((OWNERS, 1, 2 * LANES), F32),
            vmem((X, GROUP, accounts), F32),
            dma((2, X)),
            dma((2, X)),
            dma((2, X)),
            dma((2, X)),
            dma((2, X)),
            dma((2, X)),
            dma((CHUNKS, 2)),
            dma((CHUNKS, 2)),
            dma((2, Z)),
            dma((2, X)),
            dma((2,)),
            dma((2, X)),
            dma((2, X)),
        ],
        compiler_params=pltpu.CompilerParams(
            collective_id=0, has_side_effects=True, vmem_limit_bytes=58 * 2**20),
        cost_estimate=pl.CostEstimate(flops=52 * 10**9, bytes_accessed=4 * 2**20, transcendentals=0),
    )(unit_cost, upper_bound, start_primal, start_dual, net_target, owners.T, local_ids.T)
    results = (primal, duals, totals)
    primal, duals, totals = pl.pallas_call(
        finish,
        out_shape=tuple(jax.ShapeDtypeStruct(r.shape, r.dtype) for r in results),
        in_specs=[pl.BlockSpec(memory_space=vmem)] * 3,
        out_specs=[pl.BlockSpec(memory_space=vmem)] * 3,
        compiler_params=pltpu.CompilerParams(vmem_limit_bytes=60 * 2**20),
    )(*results)
    return primal, duals, totals.transpose(1, 0, 2)


def solution(mesh):
    return jax.shard_map(
        body,
        mesh=mesh,
        in_specs=(
            P("bucket", "edge"),
            P("bucket", "edge"),
            P("bucket", "edge"),
            P("bucket", "edge"),
            P("bucket", "edge"),
            P("edge", None),
            P("edge", None),
        ),
        out_specs=(P("bucket", "edge"), P("bucket", "edge"), P(None, None, "bucket")),
        check_vma=False,
    )
```

```python
import jax
import jax.numpy as jnp
from jax import lax
from jax.experimental import pallas as pl
from jax.experimental.pallas import tpu as pltpu
from jax.sharding import PartitionSpec as P

ITERS = 3
X = 4
Z = 8
OWNERS = X * Z
FAR = (4, 3, 5, 2, 6, 1, 7)
HALF = 4
CHUNKS = 2
GROUP = HALF * CHUNKS
LANES = 128
F32 = jnp.float32
BF16 = jnp.bfloat16


def turn(value):
    axis = value.ndim - 2
    first = lax.slice_in_dim(value, 0, HALF, axis=axis)
    second = lax.slice_in_dim(value, HALF, 2 * HALF, axis=axis)
    return jnp.concatenate([second, first], axis=axis)


def kernel(cost_ref, bound_ref, start_ref, dual_ref, target_ref, owner_ref, local_ref,
           primal_ref, duals_ref, totals_ref,
           cost, bound, primal, owner, local, hot, own_half, ext, left, acc,
           packed, state, gath, part, rsz, deg_part, deg_z, deg_x, step, tot, tot_all, back,
           sem_pack, sem_own, sem_loc, sem_cost, sem_bound, sem_primal, sem_agz, sem_rsz,
           sem_dz, sem_dx, sem_tot, sem_back, sem_dual, sem_here):
    edges = cost_ref.shape[1]
    slots = ITERS * CHUNKS
    me = lax.axis_index("edge")
    my_x = lax.rem(me, X)
    my_z = lax.div(me, X)
    kind = lax.broadcasted_iota(jnp.int32, (GROUP, LANES), 1) >> 5
    upper = lax.broadcasted_iota(jnp.int32, (GROUP, LANES), 0) < HALF

    def x_of(j):
        return lax.rem(my_x + j, X)

    def at_x(j):
        return my_z * X + x_of(j)

    def at_z(j):
        return lax.rem(my_z + j, Z) * X + my_x

    def group(x):
        return pl.ds(pl.multiple_of(x * GROUP, GROUP), GROUP)

    def remote(src, dst, send, recv, device):
        return pltpu.make_async_remote_copy(
            src_ref=src, dst_ref=dst, send_sem=send, recv_sem=recv,
            device_id={"edge": device}, device_id_type=pl.DeviceIdType.MESH)

    def give(src, dst, sems, j):
        return remote(src, dst.at[X - j], sems.at[0, j], sems.at[1, X - j], at_x(j))

    def give_rows(src, dst, sems, j):
        return give(src.at[group(x_of(j))], dst, sems, j)

    def taken(dst, sems, j):
        return remote(dst.at[j], dst.at[j], sems.at[0, j], sems.at[1, j], at_x(j))

    def packs(j):
        return give(packed.at[x_of(j)], state, sem_pack, j)

    def agz(c):
        block = gath.at[c, my_z]
        return [remote(block, block, sem_agz.at[c, 0], sem_agz.at[c, 1], at_z(j)) for j in FAR]

    def agz_all(c):
        blocks = gath.at[c, pl.ds(0, Z - 1)]
        return [remote(blocks, blocks, sem_agz.at[c, 0], sem_agz.at[c, 1], at_z(1))]

    def to_z(c):
        return [remote(part.at[c, lax.rem(my_z + j, Z)], rsz.at[c, j - 1], sem_rsz.at[c, 0], sem_rsz.at[c, 1], at_z(j))
                for j in FAR]

    def to_z_all(c):
        return [remote(part.at[c, pl.ds(0, Z - 1)], rsz.at[c], sem_rsz.at[c, 0], sem_rsz.at[c, 1], at_z(1))]

    def deg_to_z():
        return [remote(deg_part.at[lax.rem(my_z + j, Z)], deg_z.at[j - 1], sem_dz.at[0, j], sem_dz.at[1, j], at_z(j))
                for j in range(1, Z)]

    def deg_to_x():
        return [give(deg_x.at[0], deg_x, sem_dx, j) for j in range(1, X)]

    def tot_out(j):
        mine = tot_all.at[me]
        return remote(mine, mine, sem_tot.at[0], sem_tot.at[1], lax.rem(me + j, OWNERS))

    def tot_in():
        rows = tot_all.at[pl.ds(0, OWNERS - 1)]
        return remote(rows, rows, sem_tot.at[0], sem_tot.at[1], at_z(1))

    def primal_back(j):
        return remote(primal.at[j], primal_ref.at[group(my_x)], sem_back.at[0, j], sem_back.at[1, X - j], at_x(j))

    def dual_back(j):
        return remote(back.at[j], duals_ref.at[group(my_x)], sem_dual.at[0, j], sem_dual.at[1, X - j], at_x(j))

    def start(copies):
        for copy in copies:
            copy.start()

    def wait(copies):
        for copy in copies:
            copy.wait()

    for g in range(X):
        for which, ref in enumerate((dual_ref, target_ref)):
            rows = ref[g * GROUP:(g + 1) * GROUP, :]
            low, high = rows[:, :LANES], rows[:, LANES:]
            packed[g, 2 * which] = jnp.concatenate([low[:HALF], high[:HALF]], axis=0)
            packed[g, 2 * which + 1] = jnp.concatenate([low[HALF:], high[HALF:]], axis=0)

    def own_rows():
        return [pltpu.make_async_copy(src.at[group(my_x)], dst.at[0], sem_here.at[i])
                for i, (src, dst) in enumerate(((cost_ref, cost), (bound_ref, bound), (start_ref, primal)))]

    barrier = pltpu.get_barrier_semaphore()
    for j in range(1, OWNERS):
        pl.semaphore_signal(barrier, inc=1, device_id={"edge": lax.rem(me + j, OWNERS)},
                            device_id_type=pl.DeviceIdType.MESH)
    pl.semaphore_wait(barrier, OWNERS - 1)

    peers = (3, 1, 2)

    def give_arrays(j):
        return [give_rows(cost_ref, cost, sem_cost, j), give_rows(bound_ref, bound, sem_bound, j),
                give_rows(start_ref, primal, sem_primal, j)]

    for j in peers:
        packs(j).start()
    for j in peers:
        give(owner_ref, owner, sem_own, j).start()
        give(local_ref, local, sem_loc, j).start()

    state[0] = packed[my_x]
    owner[0] = owner_ref[...]
    local[0] = local_ref[...]
    start(own_rows())

    def build(j):
        second = lax.broadcasted_iota(jnp.int32, (2 * GROUP, 256), 0) >= GROUP

        def some(b, carry):
            here = pl.ds(pl.multiple_of(b * 256, 256), 256)
            cols = pl.ds(pl.multiple_of(j * edges + b * 256, 256), 256)
            for side in range(2):
                ids = local[j, side:side + 1, here]
                one = (lax.broadcasted_iota(jnp.int32, (256, 256), 0) == ids).astype(F32)
                hot[side, :, cols] = one.astype(BF16)
                names = jnp.broadcast_to(owner[j, side:side + 1, here], (2 * GROUP, 256))
                own_half[side, :, cols] = jnp.where(second, names - 1, names).astype(F32).astype(BF16)
            return carry

        lax.fori_loop(0, edges // 256, some, 0)

    for j in peers:
        packs(j).wait()
    for c in range(CHUNKS):
        for x in range(X):
            gath[c, my_z, x] = state[lax.rem(x + X - my_x, X), c]
        start(agz(c))
    start(give_arrays(3) + give_arrays(1))
    build(0)

    degree = None
    for side in range(2):
        rows = lax.broadcasted_iota(jnp.int32, (OWNERS, edges), 0)
        named = (rows == owner_ref[side:side + 1, :]).astype(F32).astype(BF16)
        count = lax.dot_general(named, hot[side, :, :edges], (((1,), (1,)), ((), ())), preferred_element_type=F32)
        degree = count if degree is None else degree + count
    for z in range(Z):
        four = degree[z * X:(z + 1) * X]
        deg_part[z] = jnp.concatenate([four, four], axis=0)
    start(deg_to_z())
    tot[...] = jnp.zeros_like(tot)

    for j in peers:
        give(owner_ref, owner, sem_own, j).wait()
        give(local_ref, local, sem_loc, j).wait()
    start(give_arrays(2))

    def later(j, carry):
        build(j)
        return carry

    lax.fori_loop(1, X, later, 0)

    def degree_passed():
        wait(deg_to_z())
        mine = deg_part[my_z]
        for j in range(Z - 1):
            mine = mine + deg_z[j]
        deg_x[0] = mine
        start(deg_to_x())

    def degree_done():
        wait(deg_to_x())
        whole = (deg_x[0] + deg_x[1]) + (deg_x[2] + deg_x[3])
        inverse = 1.0 / jnp.maximum(whole, 1.0)
        for x in range(X):
            low = jnp.broadcast_to(inverse[x:x + 1, :LANES], (GROUP, LANES))
            high = jnp.broadcast_to(inverse[x:x + 1, LANES:], (GROUP, LANES))
            step[x] = jnp.where(upper, low, high)

    def settle(t):
        c, sweep = lax.rem(t, CHUNKS), lax.div(t, CHUNKS)
        wait(to_z_all(c))
        squares = jnp.zeros((GROUP, LANES), F32)
        for x in range(X):
            place = lax.rem(x + X - my_x, X)
            applied = part[c, my_z, x]
            for j in range(Z - 1):
                applied = applied + rsz[c, j, x]
            residual = state[place, CHUNKS + c] - applied
            duals = state[place, c] + step[x] * residual
            state[place, c] = duals
            gath[c, my_z, x] = duals
            squares = squares + residual * residual
        square = jnp.broadcast_to(jnp.sum(squares, axis=1, keepdims=True), (GROUP, LANES))
        square = square + turn(square)
        tot[0] += jnp.where((kind == sweep) & (upper == (c == 0)), square, 0.0)

        @pl.when(sweep < ITERS - 1)
        def _():
            start(agz(c))

    def slot(t, carry):
        c, sweep = lax.rem(t, CHUNKS), lax.div(t, CHUNKS)
        wait(agz_all(c))
        value = gath[c].reshape(OWNERS, GROUP, LANES)
        high = value.astype(BF16).astype(F32)
        low = value - high
        is_upper = lax.broadcasted_iota(jnp.int32, (OWNERS, GROUP, LANES), 1) < HALF
        first = jnp.where(is_upper, high, turn(low))
        second = jnp.where(is_upper, turn(high), low)
        left[...] = jnp.concatenate([first, second], axis=2).reshape(OWNERS * GROUP, 2 * LANES).astype(BF16)
        in_upper = lax.broadcasted_iota(jnp.int32, (GROUP, edges), 0) < HALF
        in_chunk = (lax.broadcasted_iota(jnp.int32, (GROUP, edges), 0) >= HALF) == (c == 1)
        acc[...] = jnp.zeros_like(acc)

        def place(i):
            return jnp.where(i < 2, i, 5 - i)

        def pull(i, carry):
            j = place(i)

            @pl.when((t == 0) & (i > 0))
            def _():
                taken(cost, sem_cost, j).wait_recv()
                taken(bound, sem_bound, j).wait_recv()
                taken(primal, sem_primal, j).wait_recv()

            cols = pl.ds(pl.multiple_of(j * edges, edges), edges)
            ends = []
            for side in range(2):
                all_rows = jnp.dot(left[...], hot[side, :, cols], preferred_element_type=F32)
                names = jnp.broadcast_to(owner[j, side:side + 1, :], (GROUP, edges))
                found = jnp.zeros((GROUP, edges), F32)
                for o in range(OWNERS):
                    found = jnp.where(names == o, all_rows[o * GROUP:(o + 1) * GROUP], found)
                ends.append(found)
            pulled = ends[0] - ends[1]
            pulled = pulled + turn(pulled)
            price, before = cost[j], primal[j]
            moved = jnp.minimum(jnp.maximum(before - 0.5 * (price - pulled), 0.0), bound[j])
            primal[j] = jnp.where(in_chunk, moved, before)
            extended = jnp.where(in_chunk, 2.0 * moved - before, 0.0)
            extended = extended + turn(extended)
            high = extended.astype(BF16).astype(F32)
            both = jnp.where(in_upper, high, extended - high)
            both = jnp.concatenate([both, both], axis=0).astype(BF16)
            ext[0, :, cols] = both
            ext[1, :, cols] = -both
            spend = jnp.sum(jnp.where(in_chunk, price * moved, 0.0), axis=1, keepdims=True)
            tot[1] += jnp.where(kind == sweep, jnp.broadcast_to(spend, (GROUP, LANES)), 0.0)

            @pl.when((t == slots - 1) & (i > 0))
            def _():
                primal_back(j).start()

            return carry

        def push(i, carry):
            j = place(i)
            cols = pl.ds(pl.multiple_of(j * edges, edges), edges)
            for side in range(2):
                value, names = ext[side, :, cols], own_half[side, :, cols]
                zero = jnp.zeros_like(value)
                masked = jnp.concatenate(
                    [jnp.where(names == BF16(o), value, zero) for o in range(0, OWNERS, 2)], axis=0)
                acc[...] += lax.dot_general(masked, hot[side, :, cols], (((1,), (1,)), ((), ())),
                                            preferred_element_type=F32)
            return carry

        def turns(p, carry):
            low, high = jnp.where(p == 0, 0, X - 1), jnp.where((t == 0) & (p == 0), X - 1, X)
            lax.fori_loop(low, high, pull, 0)

            @pl.when(t == 1)
            def _():
                degree_done()

            @pl.when(t >= 1)
            def _():
                settle(t - 1)

            lax.fori_loop(low, high, push, 0)
            return carry

        lax.fori_loop(0, jnp.where(t == 0, 2, 1), turns, 0)
        value = acc[...].reshape(OWNERS, GROUP, 2 * LANES)
        value = value + turn(value)
        part[c] = jnp.where(is_upper, value[:, :, :LANES], value[:, :, LANES:]).reshape(Z, X, GROUP, LANES)
        start(to_z(c))

        @pl.when(t == 0)
        def _():
            degree_passed()

        return carry

    wait(own_rows())
    lax.fori_loop(0, slots, slot, 0)
    settle(slots - 1)

    lane = lax.broadcasted_iota(jnp.int32, (GROUP, LANES), 1) & (X * GROUP - 1)
    bucket = lax.broadcasted_iota(jnp.int32, (GROUP, LANES), 0) + my_x * GROUP
    for side in range(2):
        row = jnp.sum(jnp.where(lane == bucket, tot[side], 0.0), axis=0, keepdims=True)
        tot_all[me, :, side * LANES:(side + 1) * LANES] = row
    for j in range(1, OWNERS):
        tot_out(j).start()
    for j in range(X):
        first, second = state[j, 0], state[j, 1]
        back[j] = jnp.concatenate(
            [jnp.concatenate([first[:HALF], second[:HALF]], axis=0),
             jnp.concatenate([first[HALF:], second[HALF:]], axis=0)], axis=1)
    for j in peers:
        dual_back(j).start()
    duals_ref[group(my_x), :] = back[0]
    primal_ref[group(my_x), :] = primal[0]
    for j in peers:
        for copy in give_arrays(j):
            copy.wait_send()
    wait([primal_back(j) for j in peers])
    wait([dual_back(j) for j in peers])
    tot_in().wait()
    total = tot_all[0]
    for other in range(1, OWNERS):
        total = total + tot_all[other]
    for side in range(2):
        row = jnp.broadcast_to(total[:, side * LANES:(side + 1) * LANES], (GROUP, LANES))
        for i in range(ITERS):
            turned = pltpu.roll(row, (LANES - i * X * GROUP) % LANES, 1)
            totals_ref[i, side:side + 1, :] = turned[:1, :X * GROUP]


def finish(*refs):
    count = len(refs) // 2
    for i in range(count):
        refs[count + i][...] = refs[i][...]


def body(unit_cost, upper_bound, start_primal, start_dual, net_target, owners, local_ids):
    buckets, edges = unit_cost.shape
    accounts = start_dual.shape[1]
    tile = (GROUP, LANES)
    dma = pltpu.SemaphoreType.DMA
    vmem = pltpu.VMEM
    primal, duals, totals = pl.pallas_call(
        kernel,
        out_shape=(
            jax.ShapeDtypeStruct((buckets, edges), F32),
            jax.ShapeDtypeStruct((buckets, accounts), F32),
            jax.ShapeDtypeStruct((ITERS, 2, buckets), F32),
        ),
        in_specs=[pl.BlockSpec(memory_space=pl.ANY)] * 3 + [pl.BlockSpec(memory_space=vmem)] * 4,
        out_specs=[pl.BlockSpec(memory_space=vmem)] * 3,
        scratch_shapes=[
            vmem((X, GROUP, edges), F32),
            vmem((X, GROUP, edges), F32),
            vmem((X, GROUP, edges), F32),
            vmem((X, 2, edges), jnp.int32),
            vmem((X, 2, edges), jnp.int32),
            vmem((2, accounts, X * edges), BF16),
            vmem((2, 2 * GROUP, X * edges), BF16),
            vmem((2, 2 * GROUP, X * edges), BF16),
            vmem((OWNERS * GROUP, accounts), BF16),
            vmem((OWNERS * GROUP, accounts), F32),
            vmem((X, 2 * CHUNKS) + tile, F32),
            vmem((X, 2 * CHUNKS) + tile, F32),
            vmem((CHUNKS, Z, X) + tile, F32),
            vmem((CHUNKS, Z, X) + tile, F32),
            vmem((CHUNKS, Z - 1, X) + tile, F32),
            vmem((Z, GROUP, accounts), F32),
            vmem((Z - 1, GROUP, accounts), F32),
            vmem((X, GROUP, accounts), F32),
            vmem((X,) + tile, F32),
            vmem((2,) + tile, F32),
            vmem((OWNERS, 1, 2 * LANES), F32),
            vmem((X, GROUP, accounts), F32),
            dma((2, X)),
            dma((2, X)),
            dma((2, X)),
            dma((2, X)),
            dma((2, X)),
            dma((2, X)),
            dma((CHUNKS, 2)),
            dma((CHUNKS, 2)),
            dma((2, Z)),
            dma((2, X)),
            dma((2,)),
            dma((2, X)),
            dma((2, X)),
            dma((3,)),
        ],
        compiler_params=pltpu.CompilerParams(
            collective_id=0, has_side_effects=True, vmem_limit_bytes=58 * 2**20),
        cost_estimate=pl.CostEstimate(flops=52 * 10**9, bytes_accessed=4 * 2**20, transcendentals=0),
    )(unit_cost, upper_bound, start_primal, start_dual, net_target, owners.T, local_ids.T)
    results = (primal, duals, totals)
    primal, duals, totals = pl.pallas_call(
        finish,
        out_shape=tuple(jax.ShapeDtypeStruct(r.shape, r.dtype) for r in results),
        in_specs=[pl.BlockSpec(memory_space=vmem)] * 3,
        out_specs=[pl.BlockSpec(memory_space=vmem)] * 3,
        compiler_params=pltpu.CompilerParams(vmem_limit_bytes=60 * 2**20),
    )(*results)
    return primal, duals, totals.transpose(1, 0, 2)


def solution(mesh):
    return jax.shard_map(
        body,
        mesh=mesh,
        in_specs=(
            P("bucket", "edge"),
            P("bucket", "edge"),
            P("bucket", "edge"),
            P("bucket", "edge"),
            P("bucket", "edge"),
            P("edge", None),
            P("edge", None),
        ),
        out_specs=(P("bucket", "edge"), P("bucket", "edge"), P(None, None, "bucket")),
        check_vma=False,
    )
```

```python
import jax
import jax.numpy as jnp
from jax import lax
from jax.experimental import pallas as pl
from jax.experimental.pallas import tpu as pltpu
from jax.sharding import PartitionSpec as P

ITERS = 3
X = 4
Z = 8
OWNERS = X * Z
FAR = (4, 3, 5, 2, 6, 1, 7)
HALF = 4
CHUNKS = 2
GROUP = HALF * CHUNKS
LANES = 128
F32 = jnp.float32
BF16 = jnp.bfloat16


def turn(value):
    axis = value.ndim - 2
    first = lax.slice_in_dim(value, 0, HALF, axis=axis)
    second = lax.slice_in_dim(value, HALF, 2 * HALF, axis=axis)
    return jnp.concatenate([second, first], axis=axis)


def kernel(cost_ref, bound_ref, start_ref, dual_ref, target_ref, owner_ref, local_ref,
           primal_ref, duals_ref, totals_ref,
           cost, bound, primal, owner, local, hot, own_half, ext, left, acc,
           packed, state, gath, part, rsz, deg_part, deg_z, deg_x, step, tot, tot_all, back,
           sem_pack, sem_own, sem_loc, sem_cost, sem_bound, sem_primal, sem_agz, sem_rsz,
           sem_dz, sem_dx, sem_tot, sem_back, sem_dual, sem_here):
    edges = cost_ref.shape[1]
    slots = ITERS * CHUNKS
    me = lax.axis_index("edge")
    my_x = lax.rem(me, X)
    my_z = lax.div(me, X)
    kind = lax.broadcasted_iota(jnp.int32, (GROUP, LANES), 1) >> 5
    upper = lax.broadcasted_iota(jnp.int32, (GROUP, LANES), 0) < HALF

    def x_of(j):
        return lax.rem(my_x + j, X)

    def at_x(j):
        return my_z * X + x_of(j)

    def at_z(j):
        return lax.rem(my_z + j, Z) * X + my_x

    def group(x):
        return pl.ds(pl.multiple_of(x * GROUP, GROUP), GROUP)

    def remote(src, dst, send, recv, device):
        return pltpu.make_async_remote_copy(
            src_ref=src, dst_ref=dst, send_sem=send, recv_sem=recv,
            device_id={"edge": device}, device_id_type=pl.DeviceIdType.MESH)

    def give(src, dst, sems, j):
        return remote(src, dst.at[X - j], sems.at[0, j], sems.at[1, X - j], at_x(j))

    def give_rows(src, dst, sems, j):
        return give(src.at[group(x_of(j))], dst, sems, j)

    def taken(dst, sems, j):
        return remote(dst.at[j], dst.at[j], sems.at[0, j], sems.at[1, j], at_x(j))

    def packs(j):
        return give(packed.at[x_of(j)], state, sem_pack, j)

    def agz(c):
        block = gath.at[c, my_z]
        return [remote(block, block, sem_agz.at[c, 0], sem_agz.at[c, 1], at_z(j)) for j in FAR]

    def agz_all(c):
        blocks = gath.at[c, pl.ds(0, Z - 1)]
        return [remote(blocks, blocks, sem_agz.at[c, 0], sem_agz.at[c, 1], at_z(1))]

    def to_z(c):
        return [remote(part.at[c, lax.rem(my_z + j, Z)], rsz.at[c, j - 1], sem_rsz.at[c, 0], sem_rsz.at[c, 1], at_z(j))
                for j in FAR]

    def to_z_all(c):
        return [remote(part.at[c, pl.ds(0, Z - 1)], rsz.at[c], sem_rsz.at[c, 0], sem_rsz.at[c, 1], at_z(1))]

    def deg_to_z():
        return [remote(deg_part.at[lax.rem(my_z + j, Z)], deg_z.at[j - 1], sem_dz.at[0, j], sem_dz.at[1, j], at_z(j))
                for j in range(1, Z)]

    def deg_to_x():
        return [give(deg_x.at[0], deg_x, sem_dx, j) for j in range(1, X)]

    def tot_out(j):
        mine = tot_all.at[me]
        return remote(mine, mine, sem_tot.at[0], sem_tot.at[1], lax.rem(me + j, OWNERS))

    def tot_in():
        rows = tot_all.at[pl.ds(0, OWNERS - 1)]
        return remote(rows, rows, sem_tot.at[0], sem_tot.at[1], at_z(1))

    def primal_back(j):
        return remote(primal.at[j], primal_ref.at[group(my_x)], sem_back.at[0, j], sem_back.at[1, X - j], at_x(j))

    def dual_back(j):
        return remote(back.at[j], duals_ref.at[group(my_x)], sem_dual.at[0, j], sem_dual.at[1, X - j], at_x(j))

    def start(copies):
        for copy in copies:
            copy.start()

    def wait(copies):
        for copy in copies:
            copy.wait()

    for g in range(X):
        for which, ref in enumerate((dual_ref, target_ref)):
            rows = ref[g * GROUP:(g + 1) * GROUP, :]
            low, high = rows[:, :LANES], rows[:, LANES:]
            packed[g, 2 * which] = jnp.concatenate([low[:HALF], high[:HALF]], axis=0)
            packed[g, 2 * which + 1] = jnp.concatenate([low[HALF:], high[HALF:]], axis=0)

    def own_rows():
        return [pltpu.make_async_copy(src.at[group(my_x)], dst.at[0], sem_here.at[i])
                for i, (src, dst) in enumerate(((cost_ref, cost), (bound_ref, bound), (start_ref, primal)))]

    barrier = pltpu.get_barrier_semaphore()
    for j in range(1, OWNERS):
        pl.semaphore_signal(barrier, inc=1, device_id={"edge": lax.rem(me + j, OWNERS)},
                            device_id_type=pl.DeviceIdType.MESH)
    pl.semaphore_wait(barrier, OWNERS - 1)

    peers = (3, 1, 2)

    def give_arrays(j):
        return [give_rows(cost_ref, cost, sem_cost, j), give_rows(bound_ref, bound, sem_bound, j),
                give_rows(start_ref, primal, sem_primal, j)]

    for j in peers:
        packs(j).start()
    for j in peers:
        give(owner_ref, owner, sem_own, j).start()
        give(local_ref, local, sem_loc, j).start()

    state[0] = packed[my_x]
    owner[0] = owner_ref[...]
    local[0] = local_ref[...]
    start(own_rows())

    def build(j):
        second = lax.broadcasted_iota(jnp.int32, (2 * GROUP, 256), 0) >= GROUP

        def some(b, carry):
            here = pl.ds(pl.multiple_of(b * 256, 256), 256)
            cols = pl.ds(pl.multiple_of(j * edges + b * 256, 256), 256)
            for side in range(2):
                ids = local[j, side:side + 1, here]
                one = (lax.broadcasted_iota(jnp.int32, (256, 256), 0) == ids).astype(F32)
                hot[side, :, cols] = one.astype(BF16)
                names = jnp.broadcast_to(owner[j, side:side + 1, here], (2 * GROUP, 256))
                own_half[side, :, cols] = jnp.where(second, names - 1, names).astype(F32).astype(BF16)
            return carry

        lax.fori_loop(0, edges // 256, some, 0)

    for j in peers:
        packs(j).wait()
    for c in range(CHUNKS):
        for x in range(X):
            gath[c, my_z, x] = state[lax.rem(x + X - my_x, X), c]
    start(agz(0))
    start(give_arrays(3) + give_arrays(1))
    build(0)

    degree = None
    for side in range(2):
        rows = lax.broadcasted_iota(jnp.int32, (OWNERS, edges), 0)
        named = (rows == owner_ref[side:side + 1, :]).astype(F32).astype(BF16)
        count = lax.dot_general(named, hot[side, :, :edges], (((1,), (1,)), ((), ())), preferred_element_type=F32)
        degree = count if degree is None else degree + count
    for z in range(Z):
        four = degree[z * X:(z + 1) * X]
        deg_part[z] = jnp.concatenate([four, four], axis=0)
    tot[...] = jnp.zeros_like(tot)

    for j in peers:
        give(owner_ref, owner, sem_own, j).wait()
        give(local_ref, local, sem_loc, j).wait()
    start(give_arrays(2))

    def later(j, carry):
        build(j)
        return carry

    lax.fori_loop(1, X, later, 0)
    start(agz(1))
    start(deg_to_z())

    def degree_passed():
        wait(deg_to_z())
        mine = deg_part[my_z]
        for j in range(Z - 1):
            mine = mine + deg_z[j]
        deg_x[0] = mine
        start(deg_to_x())

    def degree_done():
        wait(deg_to_x())
        whole = (deg_x[0] + deg_x[1]) + (deg_x[2] + deg_x[3])
        inverse = 1.0 / jnp.maximum(whole, 1.0)
        for x in range(X):
            low = jnp.broadcast_to(inverse[x:x + 1, :LANES], (GROUP, LANES))
            high = jnp.broadcast_to(inverse[x:x + 1, LANES:], (GROUP, LANES))
            step[x] = jnp.where(upper, low, high)

    def settle(t):
        c, sweep = lax.rem(t, CHUNKS), lax.div(t, CHUNKS)
        wait(to_z_all(c))
        squares = jnp.zeros((GROUP, LANES), F32)
        for x in range(X):
            place = lax.rem(x + X - my_x, X)
            applied = part[c, my_z, x]
            for j in range(Z - 1):
                applied = applied + rsz[c, j, x]
            residual = state[place, CHUNKS + c] - applied
            duals = state[place, c] + step[x] * residual
            state[place, c] = duals
            gath[c, my_z, x] = duals
            squares = squares + residual * residual
        square = jnp.broadcast_to(jnp.sum(squares, axis=1, keepdims=True), (GROUP, LANES))
        square = square + turn(square)
        tot[0] += jnp.where((kind == sweep) & (upper == (c == 0)), square, 0.0)

        @pl.when(sweep < ITERS - 1)
        def _():
            start(agz(c))

    def slot(t, carry):
        c, sweep = lax.rem(t, CHUNKS), lax.div(t, CHUNKS)
        wait(agz_all(c))
        value = gath[c].reshape(OWNERS, GROUP, LANES)
        high = value.astype(BF16).astype(F32)
        low = value - high
        is_upper = lax.broadcasted_iota(jnp.int32, (OWNERS, GROUP, LANES), 1) < HALF
        first = jnp.where(is_upper, high, turn(low))
        second = jnp.where(is_upper, turn(high), low)
        left[...] = jnp.concatenate([first, second], axis=2).reshape(OWNERS * GROUP, 2 * LANES).astype(BF16)
        in_upper = lax.broadcasted_iota(jnp.int32, (GROUP, edges), 0) < HALF
        in_chunk = (lax.broadcasted_iota(jnp.int32, (GROUP, edges), 0) >= HALF) == (c == 1)
        acc[...] = jnp.zeros_like(acc)

        def place(i):
            return jnp.where(i < 2, i, 5 - i)

        def pull(i, carry):
            j = place(i)

            @pl.when((t == 0) & (i > 0))
            def _():
                taken(cost, sem_cost, j).wait_recv()
                taken(bound, sem_bound, j).wait_recv()
                taken(primal, sem_primal, j).wait_recv()

            cols = pl.ds(pl.multiple_of(j * edges, edges), edges)
            ends = []
            for side in range(2):
                all_rows = jnp.dot(left[...], hot[side, :, cols], preferred_element_type=F32)
                names = jnp.broadcast_to(owner[j, side:side + 1, :], (GROUP, edges))
                found = jnp.zeros((GROUP, edges), F32)
                for o in range(OWNERS):
                    found = jnp.where(names == o, all_rows[o * GROUP:(o + 1) * GROUP], found)
                ends.append(found)
            pulled = ends[0] - ends[1]
            pulled = pulled + turn(pulled)
            price, before = cost[j], primal[j]
            moved = jnp.minimum(jnp.maximum(before - 0.5 * (price - pulled), 0.0), bound[j])
            primal[j] = jnp.where(in_chunk, moved, before)
            extended = jnp.where(in_chunk, 2.0 * moved - before, 0.0)
            extended = extended + turn(extended)
            high = extended.astype(BF16).astype(F32)
            both = jnp.where(in_upper, high, extended - high)
            both = jnp.concatenate([both, both], axis=0).astype(BF16)
            ext[0, :, cols] = both
            ext[1, :, cols] = -both
            spend = jnp.sum(jnp.where(in_chunk, price * moved, 0.0), axis=1, keepdims=True)
            tot[1] += jnp.where(kind == sweep, jnp.broadcast_to(spend, (GROUP, LANES)), 0.0)

            @pl.when((t == slots - 1) & (i > 0))
            def _():
                primal_back(j).start()

            return carry

        def push(i, carry):
            j = place(i)
            cols = pl.ds(pl.multiple_of(j * edges, edges), edges)
            for side in range(2):
                value, names = ext[side, :, cols], own_half[side, :, cols]
                zero = jnp.zeros_like(value)
                masked = jnp.concatenate(
                    [jnp.where(names == BF16(o), value, zero) for o in range(0, OWNERS, 2)], axis=0)
                acc[...] += lax.dot_general(masked, hot[side, :, cols], (((1,), (1,)), ((), ())),
                                            preferred_element_type=F32)
            return carry

        def turns(p, carry):
            low, high = jnp.where(p == 0, 0, X - 1), jnp.where((t == 0) & (p == 0), X - 1, X)
            lax.fori_loop(low, high, pull, 0)

            @pl.when(t == 1)
            def _():
                degree_done()

            @pl.when(t >= 1)
            def _():
                settle(t - 1)

            lax.fori_loop(low, high, push, 0)
            return carry

        lax.fori_loop(0, jnp.where(t == 0, 2, 1), turns, 0)
        value = acc[...].reshape(OWNERS, GROUP, 2 * LANES)
        value = value + turn(value)
        part[c] = jnp.where(is_upper, value[:, :, :LANES], value[:, :, LANES:]).reshape(Z, X, GROUP, LANES)
        start(to_z(c))

        @pl.when(t == 0)
        def _():
            degree_passed()

        return carry

    wait(own_rows())
    lax.fori_loop(0, slots, slot, 0)
    settle(slots - 1)

    lane = lax.broadcasted_iota(jnp.int32, (GROUP, LANES), 1) & (X * GROUP - 1)
    bucket = lax.broadcasted_iota(jnp.int32, (GROUP, LANES), 0) + my_x * GROUP
    for side in range(2):
        row = jnp.sum(jnp.where(lane == bucket, tot[side], 0.0), axis=0, keepdims=True)
        tot_all[me, :, side * LANES:(side + 1) * LANES] = row
    for j in range(1, OWNERS):
        tot_out(j).start()
    for j in range(X):
        first, second = state[j, 0], state[j, 1]
        back[j] = jnp.concatenate(
            [jnp.concatenate([first[:HALF], second[:HALF]], axis=0),
             jnp.concatenate([first[HALF:], second[HALF:]], axis=0)], axis=1)
    for j in peers:
        dual_back(j).start()
    duals_ref[group(my_x), :] = back[0]
    primal_ref[group(my_x), :] = primal[0]
    for j in peers:
        for copy in give_arrays(j):
            copy.wait_send()
    wait([primal_back(j) for j in peers])
    wait([dual_back(j) for j in peers])
    tot_in().wait()
    total = tot_all[0]
    for other in range(1, OWNERS):
        total = total + tot_all[other]
    for side in range(2):
        row = jnp.broadcast_to(total[:, side * LANES:(side + 1) * LANES], (GROUP, LANES))
        for i in range(ITERS):
            turned = pltpu.roll(row, (LANES - i * X * GROUP) % LANES, 1)
            totals_ref[i, side:side + 1, :] = turned[:1, :X * GROUP]


def finish(*refs):
    count = len(refs) // 2
    for i in range(count):
        refs[count + i][...] = refs[i][...]


def body(unit_cost, upper_bound, start_primal, start_dual, net_target, owners, local_ids):
    buckets, edges = unit_cost.shape
    accounts = start_dual.shape[1]
    tile = (GROUP, LANES)
    dma = pltpu.SemaphoreType.DMA
    vmem = pltpu.VMEM
    primal, duals, totals = pl.pallas_call(
        kernel,
        out_shape=(
            jax.ShapeDtypeStruct((buckets, edges), F32),
            jax.ShapeDtypeStruct((buckets, accounts), F32),
            jax.ShapeDtypeStruct((ITERS, 2, buckets), F32),
        ),
        in_specs=[pl.BlockSpec(memory_space=pl.ANY)] * 3 + [pl.BlockSpec(memory_space=vmem)] * 4,
        out_specs=[pl.BlockSpec(memory_space=vmem)] * 3,
        scratch_shapes=[
            vmem((X, GROUP, edges), F32),
            vmem((X, GROUP, edges), F32),
            vmem((X, GROUP, edges), F32),
            vmem((X, 2, edges), jnp.int32),
            vmem((X, 2, edges), jnp.int32),
            vmem((2, accounts, X * edges), BF16),
            vmem((2, 2 * GROUP, X * edges), BF16),
            vmem((2, 2 * GROUP, X * edges), BF16),
            vmem((OWNERS * GROUP, accounts), BF16),
            vmem((OWNERS * GROUP, accounts), F32),
            vmem((X, 2 * CHUNKS) + tile, F32),
            vmem((X, 2 * CHUNKS) + tile, F32),
            vmem((CHUNKS, Z, X) + tile, F32),
            vmem((CHUNKS, Z, X) + tile, F32),
            vmem((CHUNKS, Z - 1, X) + tile, F32),
            vmem((Z, GROUP, accounts), F32),
            vmem((Z - 1, GROUP, accounts), F32),
            vmem((X, GROUP, accounts), F32),
            vmem((X,) + tile, F32),
            vmem((2,) + tile, F32),
            vmem((OWNERS, 1, 2 * LANES), F32),
            vmem((X, GROUP, accounts), F32),
            dma((2, X)),
            dma((2, X)),
            dma((2, X)),
            dma((2, X)),
            dma((2, X)),
            dma((2, X)),
            dma((CHUNKS, 2)),
            dma((CHUNKS, 2)),
            dma((2, Z)),
            dma((2, X)),
            dma((2,)),
            dma((2, X)),
            dma((2, X)),
            dma((3,)),
        ],
        compiler_params=pltpu.CompilerParams(
            collective_id=0, has_side_effects=True, vmem_limit_bytes=58 * 2**20),
        cost_estimate=pl.CostEstimate(flops=52 * 10**9, bytes_accessed=4 * 2**20, transcendentals=0),
    )(unit_cost, upper_bound, start_primal, start_dual, net_target, owners.T, local_ids.T)
    results = (primal, duals, totals)
    primal, duals, totals = pl.pallas_call(
        finish,
        out_shape=tuple(jax.ShapeDtypeStruct(r.shape, r.dtype) for r in results),
        in_specs=[pl.BlockSpec(memory_space=vmem)] * 3,
        out_specs=[pl.BlockSpec(memory_space=vmem)] * 3,
        compiler_params=pltpu.CompilerParams(vmem_limit_bytes=60 * 2**20),
    )(*results)
    return primal, duals, totals.transpose(1, 0, 2)


def solution(mesh):
    return jax.shard_map(
        body,
        mesh=mesh,
        in_specs=(
            P("bucket", "edge"),
            P("bucket", "edge"),
            P("bucket", "edge"),
            P("bucket", "edge"),
            P("bucket", "edge"),
            P("edge", None),
            P("edge", None),
        ),
        out_specs=(P("bucket", "edge"), P("bucket", "edge"), P(None, None, "bucket")),
        check_vma=False,
    )
```
